32 devices in a mesh: row: 4 (over x, core), col: 8 (over z, y).
Axes of the slice: x: 2, y: 2, z: 4, core: 2. Of those that a mesh axis runs over, the one named last changes fastest.
Arguments:
- grid_points: int32 [2, 12, 2048], P(None, None, 'row'), may hold values from 0 to 127
- variable: int32 [12, 2048], P(None, 'row'), may hold values from 0 to 2
Outputs:
- panel_factor: float32 [12, 2048, 1536], P(None, ('row', 'col'))
- trailing: float32 [12, 2048, 4096], P(None, 'row', 'col')
The draws below stay inside these ranges and needn't reach their ends.
All inputs are finite; a program needn't handle non-finite values.
Results may differ from the reference program's by a relative error of at most 0.0042.
Values may be sent and summed in bfloat16 or wider, within the bound.
No kernel may reach another device: no remote copies, remote signals or barrier semaphores. Data moves between devices by JAX's collectives and lax.ppermute only.
A program may use at most 128 MiB of HBM per device.

```python
import jax
import jax.numpy as jnp
from jax import lax

TILE = 512
PANELS = 3
GRID = 128
TILE_ROWS_DEV = 12
N_ROW = 4
N_COL = 8


def set_ends(array, own_key, least, top_value):
    shape = array.shape
    place = [jax.random.randint(jax.random.fold_in(own_key, axis), (), 0, shape[axis]) for axis in range(len(shape))]
    array = array.at[tuple(place)].set(least)
    longest = shape.index(max(shape))
    place[longest] = (place[longest] + 1) % shape[longest]
    return array.at[tuple(place)].set(top_value)


def setup_inputs(seed: int = 0) -> dict:
    streams_of = jax.random.split(jax.random.key(seed), 3)
    return {
        "grid_points": set_ends(jax.random.randint(streams_of[0], (2, TILE_ROWS_DEV, N_ROW * TILE), 0, GRID), jax.random.fold_in(streams_of[0], 1), 0, GRID - 1).astype(jnp.int32),
        "variable": set_ends(jax.random.randint(streams_of[1], (TILE_ROWS_DEV, N_ROW * TILE), 0, 3), jax.random.fold_in(streams_of[1], 1), 0, 2).astype(jnp.int32),
    }


range_scale = 0.05
nugget = 0.5
rho_first = 0.35
rho_second = 0.2
rho_third = 0.3
highest = lax.Precision.HIGHEST

def kind_scale(kinds):
    return jnp.where(kinds == 0, 1.0, jnp.where(kinds == 1, 1.3, 0.8))

def covariance(row_x, row_y, row_kind, col_x, col_y, col_kind):
    delta_x = (row_x[:, None] - col_x[None, :]).astype(jnp.float32)
    delta_y = (row_y[:, None] - col_y[None, :]).astype(jnp.float32)
    distance = jnp.sqrt(delta_x * delta_x + delta_y * delta_y) * (1.0 / (GRID * range_scale))
    order_sum = row_kind[:, None] + col_kind[None, :]
    dist_square = distance * distance
    dist_cube = dist_square * distance
    dist_fourth = dist_square * dist_square
    polynomial = jnp.where(order_sum == 0, 1.0, 1.0 + distance)
    polynomial = jnp.where(order_sum == 2, 1.0 + distance + dist_square / 3.0, polynomial)
    polynomial = jnp.where(order_sum == 3, 1.0 + distance + 0.4 * dist_square + dist_cube / 15.0, polynomial)
    polynomial = jnp.where(order_sum == 4, 1.0 + distance + dist_square * (3.0 / 7.0) + dist_cube * (2.0 / 21.0) + dist_fourth / 105.0, polynomial)
    correlation = jnp.where(row_kind[:, None] == col_kind[None, :], 1.0, jnp.where(order_sum == 1, rho_first, jnp.where(order_sum == 2, rho_second, rho_third)))
    scale_row = kind_scale(row_kind)
    scale_col = kind_scale(col_kind)
    return correlation * scale_row[:, None] * scale_col[None, :] * polynomial * jnp.exp(-distance)

def leading_factor(matrix, count, size):
    remaining = matrix
    lower_blocks = {}
    inverse_blocks = {}
    identity = jnp.eye(size, dtype=jnp.float32)
    for panel_step in range(count):
        row_begin = panel_step * size
        row_end = row_begin + size
        diag_factor = jnp.linalg.cholesky(remaining[row_begin:row_end, row_begin:row_end])
        diag_inverse = lax.linalg.triangular_solve(diag_factor, identity, left_side=True, lower=True)
        lower_blocks[panel_step, panel_step] = diag_factor
        inverse_blocks[panel_step, panel_step] = diag_inverse
        if panel_step + 1 < count:
            below_rows = jnp.dot(remaining[row_end:, row_begin:row_end], diag_inverse.T, precision=highest)
            for row_block in range(panel_step + 1, count):
                lower_blocks[row_block, panel_step] = below_rows[(row_block - panel_step - 1) * size:(row_block - panel_step) * size]
            trailing_part = remaining[row_end:, row_end:] - jnp.dot(below_rows, below_rows.T, precision=highest)
            remaining = remaining.at[row_end:, row_end:].set(trailing_part)
    for row_block in range(count):
        for col_block in range(row_block):
            running = jnp.zeros((size, size), jnp.float32)
            for mid_block in range(col_block, row_block):
                running = running + jnp.dot(lower_blocks[row_block, mid_block], inverse_blocks[mid_block, col_block], precision=highest)
            inverse_blocks[row_block, col_block] = -jnp.dot(inverse_blocks[row_block, row_block], running, precision=highest)
    zeros_block = jnp.zeros((size, size), jnp.float32)
    lower_rows = []
    inverse_rows = []
    for row_block in range(count):
        lower_rows.append(jnp.concatenate([lower_blocks[row_block, col_block] if col_block <= row_block else zeros_block for col_block in range(count)], 1))
        inverse_rows.append(jnp.concatenate([inverse_blocks[row_block, col_block] if col_block <= row_block else zeros_block for col_block in range(count)], 1))
    return (jnp.concatenate(lower_rows, 0), jnp.concatenate(inverse_rows, 0))

def reference(grid_points, variable):
    coord_x = grid_points[0].reshape(-1)
    coord_y = grid_points[1].reshape(-1)
    kinds = variable.reshape(-1)
    lead_size = PANELS * TILE
    order_all = coord_x.shape[0]
    lead_cov = covariance(coord_x[:lead_size], coord_y[:lead_size], kinds[:lead_size], coord_x[:lead_size], coord_y[:lead_size], kinds[:lead_size])
    lead_cov = lead_cov + nugget * jnp.eye(lead_size, dtype=jnp.float32)
    lower_factor, inverse = leading_factor(lead_cov, PANELS, TILE)
    rest_cov = covariance(coord_x[lead_size:], coord_y[lead_size:], kinds[lead_size:], coord_x[:lead_size], coord_y[:lead_size], kinds[:lead_size])
    solved = jnp.dot(rest_cov, inverse.T, precision=highest)
    panel_full = jnp.concatenate([lower_factor, solved], 0)
    panel_half = panel_full.astype(jnp.bfloat16)
    panel_wide = lax.optimization_barrier(panel_half).astype(jnp.float32)

    def column_tile(tile_index):
        col_start = lead_size + tile_index * TILE
        col_x = lax.dynamic_slice_in_dim(coord_x, col_start, TILE)
        col_y = lax.dynamic_slice_in_dim(coord_y, col_start, TILE)
        col_kind = lax.dynamic_slice_in_dim(kinds, col_start, TILE)
        cov_block = covariance(coord_x, coord_y, kinds, col_x, col_y, col_kind)
        equal = jnp.arange(order_all, dtype=jnp.int32)[:, None] == (col_start + jnp.arange(TILE, dtype=jnp.int32))[None, :]
        cov_block = jnp.where(equal, cov_block + nugget, cov_block)
        left_rows = lax.dynamic_slice_in_dim(panel_wide, col_start, TILE, 0)
        return cov_block - jnp.dot(panel_wide, left_rows.T, precision=highest)
    column_tiles = lax.map(column_tile, jnp.arange(N_COL, dtype=jnp.int32))
    trailing = jnp.transpose(column_tiles, (1, 0, 2)).reshape(order_all, N_COL * TILE)
    rows_dev = order_all // (N_ROW * TILE)
    return (panel_full.reshape(rows_dev, N_ROW * TILE, lead_size), trailing.reshape(rows_dev, N_ROW * TILE, N_COL * TILE))
```

```python
import jax
import jax.numpy as jnp
from jax import lax
from jax.experimental import pallas as pl
from jax.experimental.pallas import tpu as pltpu
from jax.sharding import PartitionSpec as P

PANELS = 3
GRID = 128
SUB = 128
BLOCK = 256
CHUNK = 32

range_scale = 0.05
nugget = 0.5
cross = ((1.0, 0.35, 0.2), (0.35, 1.0, 0.3), (0.2, 0.3, 1.0))
scales = (1.0, 1.3, 0.8)
series = (
    (1.0,),
    (1.0, 1.0),
    (1.0, 1.0, 1.0 / 3.0),
    (1.0, 1.0, 0.4, 1.0 / 15.0),
    (1.0, 1.0, 3.0 / 7.0, 2.0 / 21.0, 1.0 / 105.0),
)
log2e = 1.4426950408889634
step_scale = 1.0 / (GRID * range_scale)
f32 = jnp.float32
bf16 = jnp.bfloat16
NT = (((1,), (1,)), ((), ()))


def column_table(kinds):
    rows = []
    for kind in range(3):
        for power in range(5):
            values = []
            for other in range(3):
                terms = series[kind + other]
                base = cross[kind][other] * scales[kind] * scales[other]
                values.append(base * terms[power] * step_scale**power if power < len(terms) else 0.0)
            rows.append(
                jnp.where(kinds == 0, values[0], jnp.where(kinds == 1, values[1], values[2])).astype(f32)
            )
    rows.append(jnp.zeros_like(rows[0]))
    return jnp.stack(rows, 0)


def dot_nt(left, right):
    return lax.dot_general(left, right, NT, preferred_element_type=f32)


def dot_full(left, right, dims):
    return lax.dot_general(
        left, right, (dims, ((), ())), precision=lax.Precision.HIGHEST, preferred_element_type=f32
    )


def split_two(value):
    high = value.astype(bf16)
    return high, (value - high.astype(f32)).astype(bf16)


def split_three(value):
    high = value.astype(bf16)
    rest = value - high.astype(f32)
    mid = rest.astype(bf16)
    return high, mid, (rest - mid.astype(f32)).astype(bf16)


def covariance(row_x, row_y, row_kind, points, table, lanes):
    width = lanes.size if hasattr(lanes, "size") else lanes.stop - lanes.start
    parts = []
    for piece in range(width // 128):
        at = slice(lanes.start + 128 * piece, lanes.start + 128 * (piece + 1))
        delta_x = row_x - points[0:1, at]
        delta_y = row_y - points[1:2, at]
        square = delta_x * delta_x + delta_y * delta_y
        distance = square * lax.rsqrt(jnp.maximum(square, 1e-6))
        first = row_kind == 0.0
        second = row_kind == 1.0
        total = None
        for power in range(4, -1, -1):
            coef = jnp.where(
                first,
                table[power : power + 1, at],
                jnp.where(second, table[5 + power : 6 + power, at], table[10 + power : 11 + power, at]),
            )
            total = coef if total is None else total * distance + coef
        parts.append(total * jnp.exp2(distance * (-step_scale * log2e)))
    return jnp.concatenate(parts, 1)


def spread_row(value, index):
    return jnp.broadcast_to(value[index : index + 1, :], value.shape)


def spread_lane(value, index):
    return jnp.broadcast_to(value[:, index : index + 1], value.shape)


def inverse_factor(groups):
    count = len(groups)
    shape = groups[0].shape
    lane = lax.broadcasted_iota(jnp.int32, shape, 1)
    sub = lax.broadcasted_iota(jnp.int32, shape, 0)
    result = []
    for block in range(count):
        own = groups[block]
        columns = [spread_lane(own, 8 * block + k) for k in range(8)]
        rows = [spread_row(own, k) for k in range(8)]
        tri = {(j, k): spread_row(columns[k], j) for j in range(8) for k in range(j, 8)}
        inverse = []
        for j in range(8):
            pivot_inverse = 1.0 / tri[j, j]
            inverse.append(pivot_inverse)
            rows[j] = jnp.where(lane == 8 * block + j, tri[j, j] + 1.0, rows[j])
            for k in range(j + 1, 8):
                factor = tri[j, k] * pivot_inverse
                for m in range(k, 8):
                    tri[k, m] = tri[k, m] - factor * tri[j, m]
                rows[k] = rows[k] - factor * rows[j]
        for below in range(block + 1, count):
            column = [spread_lane(groups[below], 8 * block + k) for k in range(8)]
            value = groups[below]
            for j in range(8):
                factor = column[j] * inverse[j]
                for k in range(j + 1, 8):
                    column[k] = column[k] - factor * tri[j, k]
                value = value - factor * rows[j]
            groups[below] = value
        final, pivots = rows[0], inverse[0]
        for j in range(1, 8):
            final = jnp.where(sub == j, rows[j], final)
            pivots = jnp.where(sub == j, inverse[j], pivots)
        root = lax.sqrt(pivots)
        own_lane = 8 * block + sub
        result.append(jnp.where(lane > own_lane, 0.0, jnp.where(lane == own_lane, root, final * root)))
    return result


def kernel(
    place,
    points_rows,
    lead_points,
    lead_table,
    col_points,
    col_table,
    panel_out,
    trail_out,
    matrix,
    row_spread,
    low_high,
    low_rest,
    diag_high,
    diag_mid,
    diag_low,
    sub_inverse,
    sub_lower,
    partial,
    residual,
    rows_high,
    rows_rest,
    col_rows,
):
    step = pl.program_id(0)
    lead = lead_points.shape[1]
    tile = points_rows.shape[2]
    piece = panel_out.shape[1]
    blocks = lead // BLOCK
    row_index = place[0]
    col_index = place[1]
    row_count = place[2]
    target = place[3]

    def spread_points(points, rows):
        turned = points.T
        for which in range(3):
            row_spread[which, 0:rows, :] = jnp.broadcast_to(turned[:, which : which + 1], (rows, 128))

    @pl.when(step == 0)
    def _():
        spread_points(lead_points[...], lead)
        for j in range(blocks):
            lanes = slice(BLOCK * j, BLOCK * (j + 1))

            def fill(index, _, lanes=lanes):
                at = pl.ds(pl.multiple_of(index * CHUNK, CHUNK), CHUNK)
                value = covariance(
                    row_spread[0, at, :],
                    row_spread[1, at, :],
                    row_spread[2, at, :],
                    lead_points,
                    lead_table,
                    lanes,
                )
                row_id = lax.broadcasted_iota(jnp.int32, value.shape, 0) + index * CHUNK
                col_id = lax.broadcasted_iota(jnp.int32, value.shape, 1) + lanes.start
                matrix[at, lanes] = jnp.where(row_id == col_id, value + nugget, value)
                return 0

            lax.fori_loop(BLOCK * j // CHUNK, lead // CHUNK, fill, 0)

        def factor_step(b, _):
            base = pl.multiple_of(b * SUB, SUB)
            here = pl.ds(base, SUB)
            result = inverse_factor([matrix[pl.ds(base + 8 * i, 8), here] for i in range(SUB // 8)])
            half = lax.rem(b, 2)
            for i in range(SUB // 8):
                sub_inverse[half, 8 * i : 8 * i + 8, :] = result[i]

            @pl.when(half == 0)
            def _():
                after = pl.ds(pl.multiple_of(base + SUB, SUB), SUB)
                lower = dot_full(matrix[after, here], sub_inverse[0], ((1,), (1,)))
                sub_lower[...] = lower
                matrix[after, after] = matrix[after, after] - dot_full(lower, lower, ((1,), (1,)))

            @pl.when(half == 1)
            def _():
                t = b // 2
                corner = -dot_full(
                    sub_inverse[1],
                    dot_full(sub_lower[...], sub_inverse[0], ((1,), (0,))),
                    ((1,), (0,)),
                )
                inverse = jnp.concatenate(
                    [
                        jnp.concatenate([sub_inverse[0], jnp.zeros((SUB, SUB), f32)], 1),
                        jnp.concatenate([corner, sub_inverse[1]], 1),
                    ],
                    0,
                )
                high, mid, low = split_three(inverse)
                for copy in range(3):
                    diag_high[t, :, BLOCK * copy : BLOCK * (copy + 1)] = high
                for copy in range(2):
                    diag_mid[t, :, BLOCK * copy : BLOCK * (copy + 1)] = mid
                diag_low[t] = low
                for tt in range(blocks - 1):

                    @pl.when(t == tt)
                    def _(tt=tt):
                        begin = BLOCK * (tt + 1)
                        here = slice(BLOCK * tt, begin)
                        below_high, below_rest = split_two(matrix[begin:, here])
                        solved = (
                            dot_nt(below_high, high) + dot_nt(below_high, mid) + dot_nt(below_rest, high)
                        )
                        solved_high, solved_rest = split_two(solved)
                        low_high[begin:, here] = solved_high
                        low_rest[begin:, here] = solved_rest
                        for j in range(tt + 1, blocks):
                            stripe = slice(BLOCK * j, BLOCK * (j + 1))
                            from_row = BLOCK * j
                            matrix[from_row:, stripe] = matrix[from_row:, stripe] - (
                                dot_nt(low_high[from_row:, here], low_high[stripe, here])
                                + dot_nt(low_high[from_row:, here], low_rest[stripe, here])
                                + dot_nt(low_rest[from_row:, here], low_high[stripe, here])
                            )

            return 0

        lax.fori_loop(0, lead // SUB, factor_step, 0)

    spread_points(points_rows[0], tile)
    row_tile = jnp.where(step == 0, target, (step - 1) * row_count + row_index)
    row_start = row_tile * tile

    def own_diagonal(value, index, col_start):
        row_id = lax.broadcasted_iota(jnp.int32, value.shape, 0) + (row_start + index * CHUNK)
        col_id = lax.broadcasted_iota(jnp.int32, value.shape, 1) + col_start
        return row_id, col_id

    for t in range(blocks):
        lanes = slice(BLOCK * t, BLOCK * (t + 1))
        done = slice(0, BLOCK * t)
        if t:
            partial[:, 0:BLOCK] = (
                dot_nt(rows_high[:, done], low_high[lanes, done])
                + dot_nt(rows_high[:, done], low_rest[lanes, done])
                + dot_nt(rows_rest[:, done], low_high[lanes, done])
            )

        def remain(index, _, t=t, lanes=lanes):
            at = pl.ds(pl.multiple_of(index * CHUNK, CHUNK), CHUNK)
            value = covariance(
                row_spread[0, at, :], row_spread[1, at, :], row_spread[2, at, :], lead_points, lead_table, lanes
            )
            row_id, col_id = own_diagonal(value, index, lanes.start)
            value = jnp.where(row_id == col_id, value + nugget, value)
            if t:
                value = value - partial[at, 0:BLOCK]
            high, mid, low = split_three(value)
            residual[at, 0:BLOCK] = high
            residual[at, BLOCK : 2 * BLOCK] = mid
            residual[at, 2 * BLOCK : 3 * BLOCK] = low
            return 0

        lax.fori_loop(0, tile // CHUNK, remain, 0)
        solved = (
            dot_nt(residual[...], diag_high[t])
            + dot_nt(residual[:, 0 : 2 * BLOCK], diag_mid[t])
            + dot_nt(residual[:, 0:BLOCK], diag_low[t])
        )
        row_id = lax.broadcasted_iota(jnp.int32, solved.shape, 0) + row_start
        col_id = lax.broadcasted_iota(jnp.int32, solved.shape, 1) + lanes.start
        solved = jnp.where(col_id > row_id, 0.0, solved)
        high, rest = split_two(solved)
        rows_high[:, lanes] = high
        rows_rest[:, lanes] = rest

    @pl.when(step == 0)
    def _():
        col_rows[...] = rows_high[...]

    @pl.when(step > 0)
    def _():
        mine = pl.ds(pl.multiple_of(col_index * piece, piece), piece)
        panel_out[0] = rows_high[mine, :].astype(f32) + rows_rest[mine, :].astype(f32)
        partial[...] = dot_nt(rows_high[...], col_rows[...])
        for half in range(tile // BLOCK):
            lanes = slice(BLOCK * half, BLOCK * (half + 1))

            def finish(index, _, lanes=lanes):
                at = pl.ds(pl.multiple_of(index * CHUNK, CHUNK), CHUNK)
                value = covariance(
                    row_spread[0, at, :], row_spread[1, at, :], row_spread[2, at, :], col_points, col_table, lanes
                )
                row_id, col_id = own_diagonal(value, index, target * tile + lanes.start)
                value = jnp.where(row_id == col_id, value + nugget, value)
                trail_out[0, at, lanes] = value - partial[at, lanes]
                return 0

            lax.fori_loop(0, tile // CHUNK, finish, 0)


def local(grid_points, variable):
    slots, tile = variable.shape
    row_count = lax.axis_size("row")
    col_count = lax.axis_size("col")
    piece = tile // col_count
    row_index = lax.axis_index("row")
    col_index = lax.axis_index("col")
    lead = PANELS * tile
    blocks = lead // BLOCK
    used = -(-(PANELS + col_count) // row_count)
    own = jnp.concatenate([grid_points, variable[None]], 0)
    gathered = lax.all_gather(own[:, :used], "row", axis=2, tiled=True).reshape(3, -1)
    target = PANELS + col_index
    pad = lambda value: jnp.pad(value.astype(f32), ((0, 5), (0, 0)))
    lead_points = pad(gathered[:, :lead])
    col_values = lax.dynamic_slice_in_dim(gathered, target * tile, tile, 1)
    col_points = pad(col_values)
    lead_table = column_table(gathered[2, :lead])
    col_table = column_table(col_values[2])
    rows = jnp.concatenate([col_values[:, None], own], 1)
    points_rows = jnp.pad(jnp.transpose(rows, (1, 0, 2)).astype(f32), ((0, 0), (0, 5), (0, 0)))
    place = jnp.stack([row_index, col_index, jnp.int32(row_count), target]).astype(jnp.int32)
    whole = lambda shape: pl.BlockSpec(shape, lambda i, s: (0,) * len(shape))
    flops = 2 * (slots + 1) * tile * lead * lead * 2
    return pl.pallas_call(
        kernel,
        out_shape=(
            jax.ShapeDtypeStruct((slots, piece, lead), f32),
            jax.ShapeDtypeStruct((slots, tile, tile), f32),
        ),
        grid_spec=pltpu.PrefetchScalarGridSpec(
            num_scalar_prefetch=1,
            grid=(slots + 1,),
            in_specs=[
                pl.BlockSpec((1, 8, tile), lambda i, s: (i, 0, 0)),
                whole((8, lead)),
                whole((16, lead)),
                whole((8, tile)),
                whole((16, tile)),
            ],
            out_specs=[
                pl.BlockSpec((1, piece, lead), lambda i, s: (jnp.maximum(i - 1, 0), 0, 0)),
                pl.BlockSpec((1, tile, tile), lambda i, s: (jnp.maximum(i - 1, 0), 0, 0)),
            ],
            scratch_shapes=[
                pltpu.VMEM((lead, lead), f32),
                pltpu.VMEM((3, lead, 128), f32),
                pltpu.VMEM((lead, lead), bf16),
                pltpu.VMEM((lead, lead), bf16),
                pltpu.VMEM((blocks, BLOCK, 3 * BLOCK), bf16),
                pltpu.VMEM((blocks, BLOCK, 2 * BLOCK), bf16),
                pltpu.VMEM((blocks, BLOCK, BLOCK), bf16),
                pltpu.VMEM((2, SUB, SUB), f32),
                pltpu.VMEM((SUB, SUB), f32),
                pltpu.VMEM((tile, tile), f32),
                pltpu.VMEM((tile, 3 * BLOCK), bf16),
                pltpu.VMEM((tile, lead), bf16),
                pltpu.VMEM((tile, lead), bf16),
                pltpu.VMEM((tile, lead), bf16),
            ],
        ),
        compiler_params=pltpu.CompilerParams(
            dimension_semantics=("arbitrary",), vmem_limit_bytes=56 * 1024 * 1024
        ),
        cost_estimate=pl.CostEstimate(
            flops=flops, bytes_accessed=4 * slots * tile * (lead + tile), transcendentals=0
        ),
    )(place, points_rows, lead_points, lead_table, col_points, col_table)


def solution(mesh):
    return jax.shard_map(
        local,
        mesh=mesh,
        in_specs=(P(None, None, "row"), P(None, "row")),
        out_specs=(P(None, ("row", "col"), None), P(None, "row", "col")),
        check_vma=False,
    )
```

```python
import jax
import jax.numpy as jnp
from jax import lax
from jax.experimental import pallas as pl
from jax.experimental.pallas import tpu as pltpu
from jax.sharding import PartitionSpec as P

PANELS = 3
GRID = 128
SUB = 128
CHUNK = 32

range_scale = 0.05
nugget = 0.5
cross = ((1.0, 0.35, 0.2), (0.35, 1.0, 0.3), (0.2, 0.3, 1.0))
scales = (1.0, 1.3, 0.8)
series = (
    (1.0,),
    (1.0, 1.0),
    (1.0, 1.0, 1.0 / 3.0),
    (1.0, 1.0, 0.4, 1.0 / 15.0),
    (1.0, 1.0, 3.0 / 7.0, 2.0 / 21.0, 1.0 / 105.0),
)
log2e = 1.4426950408889634
step_scale = 1.0 / (GRID * range_scale)
f32 = jnp.float32
bf16 = jnp.bfloat16
NT = (((1,), (1,)), ((), ()))


def column_table(kinds):
    rows = []
    for kind in range(3):
        for power in range(5):
            values = []
            for other in range(3):
                terms = series[kind + other]
                base = cross[kind][other] * scales[kind] * scales[other]
                values.append(base * terms[power] * step_scale**power if power < len(terms) else 0.0)
            rows.append(
                jnp.where(kinds == 0, values[0], jnp.where(kinds == 1, values[1], values[2])).astype(f32)
            )
    rows.append(jnp.zeros_like(rows[0]))
    return jnp.stack(rows, 0)


def dot_nt(left, right):
    return lax.dot_general(left, right, NT, preferred_element_type=f32)


def dot_full(left, right, dims):
    return lax.dot_general(
        left, right, (dims, ((), ())), precision=lax.Precision.HIGHEST, preferred_element_type=f32
    )


def split_two(value):
    high = value.astype(bf16)
    return high, (value - high.astype(f32)).astype(bf16)


def split_three(value):
    high = value.astype(bf16)
    rest = value - high.astype(f32)
    mid = rest.astype(bf16)
    return high, mid, (rest - mid.astype(f32)).astype(bf16)


def covariance(spread, rows, points, table, lanes):
    delta_x = spread[0, rows, :] - points[0:1, lanes]
    delta_y = spread[1, rows, :] - points[1:2, lanes]
    kind = spread[2, rows, :]
    square = delta_x * delta_x + delta_y * delta_y
    distance = square * lax.rsqrt(jnp.maximum(square, 1e-6))
    total = None
    for power in range(4, -1, -1):
        coef = jnp.where(
            kind == 0.0,
            table[power : power + 1, lanes],
            jnp.where(kind == 1.0, table[5 + power : 6 + power, lanes], table[10 + power : 11 + power, lanes]),
        )
        total = coef if total is None else total * distance + coef
    return total * jnp.exp2(distance * (-step_scale * log2e))


def spread_row(value, index):
    return jnp.broadcast_to(value[index : index + 1, :], value.shape)


def spread_lane(value, index):
    return jnp.broadcast_to(value[:, index : index + 1], value.shape)


def inverse_factor(groups):
    count = len(groups)
    shape = groups[0].shape
    lane = lax.broadcasted_iota(jnp.int32, shape, 1)
    sub = lax.broadcasted_iota(jnp.int32, shape, 0)
    result = []
    for block in range(count):
        own = groups[block]
        columns = [spread_lane(own, 8 * block + k) for k in range(8)]
        rows = [spread_row(own, k) for k in range(8)]
        tri = {(j, k): spread_row(columns[k], j) for j in range(8) for k in range(j, 8)}
        inverse = []
        for j in range(8):
            pivot_inverse = 1.0 / tri[j, j]
            inverse.append(pivot_inverse)
            rows[j] = jnp.where(lane == 8 * block + j, tri[j, j] + 1.0, rows[j])
            for k in range(j + 1, 8):
                factor = tri[j, k] * pivot_inverse
                for m in range(k, 8):
                    tri[k, m] = tri[k, m] - factor * tri[j, m]
                rows[k] = rows[k] - factor * rows[j]
        for below in range(block + 1, count):
            column = [spread_lane(groups[below], 8 * block + k) for k in range(8)]
            value = groups[below]
            for j in range(8):
                factor = column[j] * inverse[j]
                for k in range(j + 1, 8):
                    column[k] = column[k] - factor * tri[j, k]
                value = value - factor * rows[j]
            groups[below] = value
        final, pivots = rows[0], inverse[0]
        for j in range(1, 8):
            final = jnp.where(sub == j, rows[j], final)
            pivots = jnp.where(sub == j, inverse[j], pivots)
        root = lax.sqrt(pivots)
        own_lane = 8 * block + sub
        result.append(jnp.where(lane > own_lane, 0.0, jnp.where(lane == own_lane, root, final * root)))
    return result


def kernel(
    place,
    points_rows,
    points_next,
    lead_points,
    lead_table,
    col_points,
    col_table,
    panel_out,
    trail_out,
    matrix,
    row_spread,
    low_pieces,
    diag_first,
    diag_second,
    step_high,
    step_rest,
    sub_inverse,
    sub_lower,
    block_inverse,
    block_lower,
    cov_ahead,
    residual,
    rows_pieces,
    col_rows,
):
    step = pl.program_id(0)
    lead = lead_points.shape[1]
    tile = points_rows.shape[2]
    piece = panel_out.shape[1]
    half_tile = tile // 2
    panels = lead // tile
    blocks = lead // half_tile
    row_index = place[0]
    col_index = place[1]
    row_count = place[2]
    target = place[3]
    chunks = [slice(CHUNK * i, CHUNK * (i + 1)) for i in range(tile // CHUNK)]

    def spread_points(points, rows):
        turned = points.T
        for which in range(3):
            row_spread[which, 0:rows, :] = jnp.broadcast_to(turned[:, which : which + 1], (rows, 128))

    def cov_block(points, table, begin, slot):
        for start in range(0, tile, 128):
            for rows in chunks:
                cov_ahead[slot, rows, start : start + 128] = covariance(
                    row_spread, rows, points, table, slice(begin + start, begin + start + 128)
                )

    def cov_loop(points, table, begin, slot):
        def body(index, _):
            rows = pl.ds(pl.multiple_of(index * 128, 128), 128)
            for start in range(0, tile, 128):
                cov_ahead[slot, rows, start : start + 128] = covariance(
                    row_spread, rows, points, table, slice(begin + start, begin + start + 128)
                )
            return 0

        lax.fori_loop(0, tile // 128, body, 0)

    def add_diagonal(slot):
        for start in range(0, tile, 128):
            here = slice(start, start + 128)
            row_id = lax.broadcasted_iota(jnp.int32, (128, 128), 0)
            col_id = lax.broadcasted_iota(jnp.int32, (128, 128), 1)
            cov_ahead[slot, here, here] = cov_ahead[slot, here, here] + jnp.where(row_id == col_id, nugget, 0.0)

    @pl.when(step == 0)
    def _():
        spread_points(lead_points[...], lead)
        for j in range(blocks):
            begin = half_tile * j

            def fill(index, _, begin=begin):
                at = pl.ds(pl.multiple_of(index * 128, 128), 128)
                for start in range(begin, begin + half_tile, 128):
                    value = covariance(row_spread, at, lead_points, lead_table, slice(start, start + 128))
                    row_id = lax.broadcasted_iota(jnp.int32, value.shape, 0) + index * 128
                    col_id = lax.broadcasted_iota(jnp.int32, value.shape, 1) + start
                    matrix[at, start : start + 128] = jnp.where(row_id == col_id, value + nugget, value)
                return 0

            lax.fori_loop(begin // 128, lead // 128, fill, 0)

        def factor_step(b, _):
            base = pl.multiple_of(b * SUB, SUB)
            here = pl.ds(base, SUB)
            result = inverse_factor([matrix[pl.ds(base + 8 * i, 8), here] for i in range(SUB // 8)])
            half = lax.rem(b, 2)
            for i in range(SUB // 8):
                sub_inverse[half, 8 * i : 8 * i + 8, :] = result[i]

            @pl.when(half == 0)
            def _():
                after = pl.ds(pl.multiple_of(base + SUB, SUB), SUB)
                lower = dot_full(matrix[after, here], sub_inverse[0], ((1,), (1,)))
                sub_lower[...] = lower
                matrix[after, after] = matrix[after, after] - dot_full(lower, lower, ((1,), (1,)))

            @pl.when(half == 1)
            def _():
                block = b // 2
                parity = lax.rem(block, 2)
                corner = -dot_full(
                    sub_inverse[1],
                    dot_full(sub_lower[...], sub_inverse[0], ((1,), (0,))),
                    ((1,), (0,)),
                )
                inverse = jnp.concatenate(
                    [
                        jnp.concatenate([sub_inverse[0], jnp.zeros((SUB, SUB), f32)], 1),
                        jnp.concatenate([corner, sub_inverse[1]], 1),
                    ],
                    0,
                )
                block_inverse[parity] = inverse
                high, mid = split_two(inverse)
                for which in range(blocks):

                    @pl.when(block == which)
                    def _(which=which):
                        begin = half_tile * (which + 1)
                        here = slice(half_tile * which, begin)
                        panel, odd = which // 2, which % 2
                        if begin < lead:
                            below_high, below_rest = split_two(matrix[begin:, here])
                            solved = (
                                dot_nt(below_high, high) + dot_nt(below_high, mid) + dot_nt(below_rest, high)
                            )
                            solved_high, solved_rest = split_two(solved)
                            step_high[begin:, :] = solved_high
                            step_rest[begin:, :] = solved_rest
                            for j in range(which + 1, blocks):
                                stripe = slice(half_tile * j, half_tile * (j + 1))
                                from_row = half_tile * j
                                matrix[from_row:, stripe] = matrix[from_row:, stripe] - (
                                    dot_nt(step_high[from_row:, :], step_high[stripe, :])
                                    + dot_nt(step_high[from_row:, :], step_rest[stripe, :])
                                    + dot_nt(step_rest[from_row:, :], step_high[stripe, :])
                                )
                            later = slice(tile * (panel + 1), lead)
                            if panel + 1 < panels:
                                at = 3 * tile * panel + half_tile * odd
                                low_pieces[later, at : at + half_tile] = step_high[later, :]
                                low_pieces[later, at + tile : at + tile + half_tile] = step_rest[later, :]
                                low_pieces[later, at + 2 * tile : at + 2 * tile + half_tile] = step_high[later, :]
                            if odd == 0:
                                block_lower[...] = solved[0:half_tile, :]
                        if odd == 1:
                            cross_part = -dot_full(
                                block_inverse[1],
                                dot_full(block_lower[...], block_inverse[0], ((1,), (0,))),
                                ((1,), (0,)),
                            )
                            first = split_three(block_inverse[0])
                            second = split_three(cross_part), split_three(block_inverse[1])
                            for order, kind in enumerate((0, 1, 2, 0, 1, 0)):
                                at = slice(half_tile * order, half_tile * (order + 1))
                                diag_first[panel, :, at] = first[kind]
                                for group in range(2):
                                    at = slice(
                                        half_tile * (6 * group + order), half_tile * (6 * group + order + 1)
                                    )
                                    diag_second[panel, :, at] = second[group][kind]

            return 0

        lax.fori_loop(0, lead // SUB, factor_step, 0)
        spread_points(points_rows[0], tile)
        cov_loop(lead_points, lead_table, 0, 0)

    row_tile = jnp.where(step == 0, target, (step - 1) * row_count + row_index)
    always = step >= 0

    for t in range(panels):

        @pl.when(row_tile == t)
        def _(t=t):
            add_diagonal(t % 2)

        @pl.when(always)
        def _(t=t):
            known = None
            if t:
                known = dot_nt(
                    rows_pieces[:, 0 : 3 * tile * t], low_pieces[tile * t : tile * (t + 1), 0 : 3 * tile * t]
                )
            for start in range(0, tile, 128):
                lanes = slice(start, start + 128)
                for rows in chunks:
                    value = cov_ahead[t % 2, rows, lanes]
                    if t:
                        value = value - known[rows, lanes]
                    pieces = split_three(value)
                    at = start if start < half_tile else start + 5 * half_tile
                    for order, kind in enumerate((0, 0, 0, 1, 1, 2)):
                        residual[rows, at + half_tile * order : at + half_tile * order + 128] = pieces[kind]
            for half, diag in enumerate((diag_first, diag_second)):
                solved = dot_nt(residual[:, 0 : 6 * half_tile * (half + 1)], diag[t])
                high, rest = split_two(solved)
                at = 3 * tile * t + half_tile * half
                rows_pieces[:, at : at + half_tile] = high
                if t + 1 < panels:
                    rows_pieces[:, at + tile : at + tile + half_tile] = high
                rows_pieces[:, at + 2 * tile : at + 2 * tile + half_tile] = rest
            if t + 1 < panels:
                cov_block(lead_points, lead_table, tile * (t + 1), (t + 1) % 2)
            else:
                cov_block(col_points, col_table, 0, (t + 1) % 2)

        @pl.when(row_tile <= t)
        def _(t=t):
            for order in (0, 1, 2):
                at = slice(tile * (3 * t + order), tile * (3 * t + order + 1))
                for start in range(0, tile, 128):
                    rows = slice(start, start + 128)
                    value = rows_pieces[rows, at]
                    row_id = lax.broadcasted_iota(jnp.int32, value.shape, 0) + start + row_tile * tile
                    col_id = lax.broadcasted_iota(jnp.int32, value.shape, 1) + t * tile
                    rows_pieces[rows, at] = jnp.where(col_id > row_id, jnp.zeros_like(value), value)

    last = panels % 2

    @pl.when(step == 0)
    def _():
        for t in range(panels):
            col_rows[:, tile * t : tile * (t + 1)] = rows_pieces[:, 3 * tile * t : 3 * tile * t + tile]
        spread_points(points_next[0], tile)
        cov_loop(lead_points, lead_table, 0, 0)

    @pl.when((step > 0) & (row_tile == target))
    def _():
        add_diagonal(last)

    @pl.when(step > 0)
    def _():
        mine = pl.ds(pl.multiple_of(col_index * piece, piece), piece)
        update = None
        for t in range(panels):
            at = 3 * tile * t
            high = rows_pieces[mine, at : at + tile].astype(f32)
            rest = rows_pieces[mine, at + 2 * tile : at + 3 * tile].astype(f32)
            panel_out[0, :, tile * t : tile * (t + 1)] = high + rest
            term = dot_nt(rows_pieces[:, at : at + tile], col_rows[:, tile * t : tile * (t + 1)])
            update = term if update is None else update + term
        for start in range(0, tile, 128):
            lanes = slice(start, start + 128)
            for rows in chunks:
                trail_out[0, rows, lanes] = cov_ahead[last, rows, lanes] - update[rows, lanes]
        spread_points(points_next[0], tile)
        cov_block(lead_points, lead_table, 0, 0)


def local(grid_points, variable):
    slots, tile = variable.shape
    row_count = lax.axis_size("row")
    col_count = lax.axis_size("col")
    piece = tile // col_count
    row_index = lax.axis_index("row")
    col_index = lax.axis_index("col")
    lead = PANELS * tile
    used = -(-(PANELS + col_count) // row_count)
    own = jnp.concatenate([grid_points, variable[None]], 0)
    gathered = lax.all_gather(own[:, :used], "row", axis=2, tiled=True).reshape(3, -1)
    target = PANELS + col_index
    pad = lambda value: jnp.pad(value.astype(f32), ((0, 5), (0, 0)))
    lead_points = pad(gathered[:, :lead])
    col_values = lax.dynamic_slice_in_dim(gathered, target * tile, tile, 1)
    col_points = pad(col_values)
    lead_table = column_table(gathered[2, :lead])
    col_table = column_table(col_values[2])
    rows = jnp.concatenate([col_values[:, None], own], 1)
    points_rows = jnp.pad(jnp.transpose(rows, (1, 0, 2)).astype(f32), ((0, 0), (0, 5), (0, 0)))
    place = jnp.stack([row_index, col_index, jnp.int32(row_count), target]).astype(jnp.int32)
    whole = lambda shape: pl.BlockSpec(shape, lambda i, s: (0,) * len(shape))
    half_tile = tile // 2
    flops = 2 * (slots + 1) * tile * lead * lead * 3
    return pl.pallas_call(
        kernel,
        out_shape=(
            jax.ShapeDtypeStruct((slots, piece, lead), f32),
            jax.ShapeDtypeStruct((slots, tile, tile), f32),
        ),
        grid_spec=pltpu.PrefetchScalarGridSpec(
            num_scalar_prefetch=1,
            grid=(slots + 1,),
            in_specs=[
                pl.BlockSpec((1, 8, tile), lambda i, s: (i, 0, 0)),
                pl.BlockSpec((1, 8, tile), lambda i, s: (jnp.minimum(i + 1, slots), 0, 0)),
                whole((8, lead)),
                whole((16, lead)),
                whole((8, tile)),
                whole((16, tile)),
            ],
            out_specs=[
                pl.BlockSpec((1, piece, lead), lambda i, s: (jnp.maximum(i - 1, 0), 0, 0)),
                pl.BlockSpec((1, tile, tile), lambda i, s: (jnp.maximum(i - 1, 0), 0, 0)),
            ],
            scratch_shapes=[
                pltpu.VMEM((lead, lead), f32),
                pltpu.VMEM((3, lead, 128), f32),
                pltpu.VMEM((lead, 3 * (lead - tile)), bf16),
                pltpu.VMEM((PANELS, half_tile, 6 * half_tile), bf16),
                pltpu.VMEM((PANELS, half_tile, 12 * half_tile), bf16),
                pltpu.VMEM((lead, half_tile), bf16),
                pltpu.VMEM((lead, half_tile), bf16),
                pltpu.VMEM((2, SUB, SUB), f32),
                pltpu.VMEM((SUB, SUB), f32),
                pltpu.VMEM((2, half_tile, half_tile), f32),
                pltpu.VMEM((half_tile, half_tile), f32),
                pltpu.VMEM((2, tile, tile), f32),
                pltpu.VMEM((tile, 12 * half_tile), bf16),
                pltpu.VMEM((tile, 3 * lead), bf16),
                pltpu.VMEM((tile, lead), bf16),
            ],
        ),
        compiler_params=pltpu.CompilerParams(
            dimension_semantics=("arbitrary",), vmem_limit_bytes=58 * 1024 * 1024
        ),
        cost_estimate=pl.CostEstimate(
            flops=flops, bytes_accessed=4 * slots * tile * (lead + tile), transcendentals=0
        ),
    )(place, points_rows, points_rows, lead_points, lead_table, col_points, col_table)


def solution(mesh):
    return jax.shard_map(
        local,
        mesh=mesh,
        in_specs=(P(None, None, "row"), P(None, "row")),
        out_specs=(P(None, ("row", "col"), None), P(None, "row", "col")),
        check_vma=False,
    )
```

```python
import functools
import math

import jax
import jax.numpy as jnp
from jax import lax
from jax.experimental import pallas as pl
from jax.experimental.pallas import tpu as pltpu
from jax.sharding import PartitionSpec as P

PANELS = 3
GRID = 128
SUB = 128
CHUNK = 32
PART = 256
SHARE = 3

range_scale = 0.05
nugget = 0.5
cross = ((1.0, 0.35, 0.2), (0.35, 1.0, 0.3), (0.2, 0.3, 1.0))
scales = (1.0, 1.3, 0.8)
series = (
    (1.0,),
    (1.0, 1.0),
    (1.0, 1.0, 1.0 / 3.0),
    (1.0, 1.0, 0.4, 1.0 / 15.0),
    (1.0, 1.0, 3.0 / 7.0, 2.0 / 21.0, 1.0 / 105.0),
)
log2e = 1.4426950408889634
step_scale = 1.0 / (GRID * range_scale)
f32 = jnp.float32
bf16 = jnp.bfloat16
NT = (((1,), (1,)), ((), ()))


def column_table(kinds):
    rows = []
    for kind in range(3):
        for power in range(5):
            values = []
            for other in range(3):
                terms = series[kind + other]
                base = cross[kind][other] * scales[kind] * scales[other]
                values.append(base * terms[power] * step_scale**power if power < len(terms) else 0.0)
            rows.append(
                jnp.where(kinds == 0, values[0], jnp.where(kinds == 1, values[1], values[2])).astype(f32)
            )
    rows.append(jnp.zeros_like(rows[0]))
    return jnp.stack(rows, 0)


def dot_nt(left, right):
    return lax.dot_general(left, right, NT, preferred_element_type=f32)


def dot_full(left, right, dims):
    return lax.dot_general(
        left, right, (dims, ((), ())), precision=lax.Precision.HIGHEST, preferred_element_type=f32
    )


def split_two(value):
    high = value.astype(bf16)
    return high, (value - high.astype(f32)).astype(bf16)


def split_three(value):
    high = value.astype(bf16)
    rest = value - high.astype(f32)
    mid = rest.astype(bf16)
    return high, mid, (rest - mid.astype(f32)).astype(bf16)


def covariance(spread, rows, points, table, lanes):
    delta_x = spread[0, rows, :] - points[0:1, lanes]
    delta_y = spread[1, rows, :] - points[1:2, lanes]
    kind = spread[2, rows, :]
    square = delta_x * delta_x + delta_y * delta_y
    distance = square * lax.rsqrt(jnp.maximum(square, 1e-6))
    total = None
    for power in range(4, -1, -1):
        coef = jnp.where(
            kind == 0.0,
            table[power : power + 1, lanes],
            jnp.where(kind == 1.0, table[5 + power : 6 + power, lanes], table[10 + power : 11 + power, lanes]),
        )
        total = coef if total is None else total * distance + coef
    return total * jnp.exp2(distance * (-step_scale * log2e))


def spread_row(value, index):
    return jnp.broadcast_to(value[index : index + 1, :], value.shape)


def spread_lane(value, index):
    return jnp.broadcast_to(value[:, index : index + 1], value.shape)


def inverse_factor(groups):
    count = len(groups)
    shape = groups[0].shape
    lane = lax.broadcasted_iota(jnp.int32, shape, 1)
    sub = lax.broadcasted_iota(jnp.int32, shape, 0)
    result = []
    for block in range(count):
        own = groups[block]
        columns = [spread_lane(own, 8 * block + k) for k in range(8)]
        rows = [spread_row(own, k) for k in range(8)]
        tri = {(j, k): spread_row(columns[k], j) for j in range(8) for k in range(j, 8)}
        inverse = []
        for j in range(8):
            if j % 2 == 0:
                second = tri[j, j] * tri[j + 1, j + 1] - tri[j, j + 1] * tri[j, j + 1]
                inverse += [1.0 / tri[j, j], tri[j, j] * (1.0 / second)]
            rows[j] = jnp.where(lane == 8 * block + j, tri[j, j] + 1.0, rows[j])
            for k in range(j + 1, 8):
                factor = tri[j, k] * inverse[j]
                for m in range(k, 8):
                    tri[k, m] = tri[k, m] - factor * tri[j, m]
                rows[k] = rows[k] - factor * rows[j]
        for below in range(block + 1, count):
            column = [spread_lane(groups[below], 8 * block + k) for k in range(8)]
            value = groups[below]
            for j in range(8):
                factor = column[j] * inverse[j]
                for k in range(j + 1, 8):
                    column[k] = column[k] - factor * tri[j, k]
                value = value - factor * rows[j]
            groups[below] = value
        final, pivots = rows[0], inverse[0]
        for j in range(1, 8):
            final = jnp.where(sub == j, rows[j], final)
            pivots = jnp.where(sub == j, inverse[j], pivots)
        root = lax.sqrt(pivots)
        own_lane = 8 * block + sub
        result.append(jnp.where(lane > own_lane, 0.0, jnp.where(lane == own_lane, root, final * root)))
    return result


def spread_points(points, spread):
    rows = points.shape[1]
    turned = points.T
    for which in range(3):
        spread[which, 0:rows, :] = jnp.broadcast_to(turned[:, which : which + 1], (rows, 128))


def covariance_loop(spread, points, table, out, rows_count, width):
    def body(index, _):
        rows = pl.ds(pl.multiple_of(index * 128, 128), 128)
        for start in range(0, width, 128):
            out[rows, start : start + 128] = covariance(spread, rows, points, table, slice(start, start + 128))
        return 0

    lax.fori_loop(0, rows_count // 128, body, 0)


def add_diagonal(block):
    for start in range(0, block.shape[0], 128):
        here = slice(start, start + 128)
        row_id = lax.broadcasted_iota(jnp.int32, (128, 128), 0)
        col_id = lax.broadcasted_iota(jnp.int32, (128, 128), 1)
        block[here, here] = block[here, here] + jnp.where(row_id == col_id, nugget, 0.0)


class Ahead:
    def __init__(self, spread, points, table, begin, out):
        self.args = (spread, points, table, begin, out)
        rows, width = out.shape
        self.units = [
            (start, slice(row, row + CHUNK)) for start in range(0, width, 128) for row in range(0, rows, CHUNK)
        ]
        self.total = len(self.units)

    def share(self, part):
        spread, points, table, begin, out = self.args
        for _ in range(min(len(self.units), math.ceil(self.total * part))):
            start, rows = self.units.pop(0)
            out[rows, start : start + 128] = covariance(
                spread, rows, points, table, slice(begin + start, begin + start + 128)
            )


def row_parts(count):
    return [slice(start, min(start + PART, count)) for start in range(0, count, PART)]


def expand(low, diag, low_pieces, diag_first, diag_second):
    panels, half_tile, _ = diag_first.shape
    tile = 2 * half_tile
    rest_at = low.shape[1] // 2
    for panel in range(panels - 1):
        own = slice(tile * panel, tile * (panel + 1))
        other = slice(rest_at + tile * panel, rest_at + tile * (panel + 1))
        for order, source in enumerate((own, other, own)):
            at = tile * (3 * panel + order)
            low_pieces[tile * panel :, at : at + tile] = low[tile * panel :, source]
    for panel in range(panels):
        for order, kind in enumerate((0, 1, 2, 0, 1, 0)):
            for group in range(3):
                source = slice(half_tile * (3 * group + kind), half_tile * (3 * group + kind + 1))
                place = order if group == 0 else 6 * (group - 1) + order
                at = slice(half_tile * place, half_tile * (place + 1))
                (diag_first if group == 0 else diag_second)[panel, :, at] = diag[panel, :, source]


def solve_block(t, cov, low_pieces, diag_first, diag_second, residual, rows_pieces, ahead):
    panels, half_tile, _ = diag_first.shape
    tile = 2 * half_tile
    parts = row_parts(cov.shape[0])
    portion = 0.25 / len(parts)
    for part in parts:
        known = None
        if t:
            known = dot_nt(rows_pieces[part, 0 : 3 * tile * t], low_pieces[tile * (t - 1) : tile * t, 0 : 3 * tile * t])
        ahead.share(portion)
        for start in range(0, tile, 128):
            lanes = slice(start, start + 128)
            for row in range(part.start, part.stop, CHUNK):
                rows = slice(row, row + CHUNK)
                value = cov[rows, lanes]
                if t:
                    value = value - known[row - part.start : row - part.start + CHUNK, lanes]
                pieces = split_three(value)
                at = start if start < half_tile else start + 5 * half_tile
                for order, kind in enumerate((0, 0, 0, 1, 1, 2)):
                    residual[rows, at + half_tile * order : at + half_tile * order + 128] = pieces[kind]
        ahead.share(portion)
    for part in parts:
        for half, diag in enumerate((diag_first, diag_second)):
            solved = dot_nt(residual[part, 0 : 6 * half_tile * (half + 1)], diag[t])
            ahead.share(portion)
            high, rest = split_two(solved)
            at = 3 * tile * t + half_tile * half
            rows_pieces[part, at : at + half_tile] = high
            if t + 1 < panels:
                rows_pieces[part, at + tile : at + tile + half_tile] = high
            rows_pieces[part, at + 2 * tile : at + 2 * tile + half_tile] = rest
    ahead.share(1.0)


class Nothing:
    def share(self, part):
        pass


def factor_kernel(
    points_rows,
    lead_points,
    lead_table,
    panel_out,
    low,
    diag,
    col_rows,
    shared_rows,
    matrix,
    row_spread,
    low_pieces,
    diag_first,
    diag_second,
    step_high,
    step_rest,
    sub_inverse,
    sub_lower,
    block_inverse,
    block_lower,
    cov_even,
    cov_odd,
    residual,
    rows_pieces,
):
    lead = lead_points.shape[1]
    tile = col_rows.shape[0]
    count = points_rows.shape[1]
    shared, piece, _ = panel_out.shape
    half_tile = tile // 2
    panels = lead // tile
    blocks = lead // half_tile
    rest_at = lead - tile
    spread_points(lead_points[...], row_spread)
    for j in range(blocks):
        begin = half_tile * j

        def fill(index, _, begin=begin):
            at = pl.ds(pl.multiple_of(index * 128, 128), 128)
            for start in range(begin, begin + half_tile, 128):
                value = covariance(row_spread, at, lead_points, lead_table, slice(start, start + 128))
                row_id = lax.broadcasted_iota(jnp.int32, value.shape, 0) + index * 128
                col_id = lax.broadcasted_iota(jnp.int32, value.shape, 1) + start
                matrix[at, start : start + 128] = jnp.where(row_id == col_id, value + nugget, value)
            return 0

        lax.fori_loop(begin // 128, lead // 128, fill, 0)

    def factor_step(b, _):
        base = pl.multiple_of(b * SUB, SUB)
        here = pl.ds(base, SUB)
        result = inverse_factor([matrix[pl.ds(base + 8 * i, 8), here] for i in range(SUB // 8)])
        half = lax.rem(b, 2)
        for i in range(SUB // 8):
            sub_inverse[half, 8 * i : 8 * i + 8, :] = result[i]

        @pl.when(half == 0)
        def _():
            after = pl.ds(pl.multiple_of(base + SUB, SUB), SUB)
            lower = dot_full(matrix[after, here], sub_inverse[0], ((1,), (1,)))
            sub_lower[...] = lower
            matrix[after, after] = matrix[after, after] - dot_full(lower, lower, ((1,), (1,)))

        @pl.when(half == 1)
        def _():
            block = b // 2
            parity = lax.rem(block, 2)
            corner = -dot_full(
                sub_inverse[1],
                dot_full(sub_lower[...], sub_inverse[0], ((1,), (0,))),
                ((1,), (0,)),
            )
            inverse = jnp.concatenate(
                [
                    jnp.concatenate([sub_inverse[0], jnp.zeros((SUB, SUB), f32)], 1),
                    jnp.concatenate([corner, sub_inverse[1]], 1),
                ],
                0,
            )
            block_inverse[parity] = inverse
            high, mid = split_two(inverse)
            for which in range(blocks):

                @pl.when(block == which)
                def _(which=which):
                    begin = half_tile * (which + 1)
                    here = slice(half_tile * which, begin)
                    panel, odd = which // 2, which % 2
                    if begin < lead:
                        below_high, below_rest = split_two(matrix[begin:, here])
                        solved = dot_nt(below_high, high) + dot_nt(below_high, mid) + dot_nt(below_rest, high)
                        solved_high, solved_rest = split_two(solved)
                        step_high[begin:, :] = solved_high
                        step_rest[begin:, :] = solved_rest
                        for j in range(which + 1, blocks):
                            stripe = slice(half_tile * j, half_tile * (j + 1))
                            from_row = half_tile * j
                            matrix[from_row:, stripe] = matrix[from_row:, stripe] - (
                                dot_nt(step_high[from_row:, :], step_high[stripe, :])
                                + dot_nt(step_high[from_row:, :], step_rest[stripe, :])
                                + dot_nt(step_rest[from_row:, :], step_high[stripe, :])
                            )
                        if panel + 1 < panels:
                            later = slice(tile * (panel + 1), lead)
                            target = slice(tile * panel, lead - tile)
                            low[target, here] = step_high[later, :]
                            low[target, rest_at + here.start : rest_at + here.stop] = step_rest[later, :]
                        if odd == 0:
                            block_lower[...] = solved[0:half_tile, :]
                    if odd == 1:
                        cross_part = -dot_full(
                            block_inverse[1],
                            dot_full(block_lower[...], block_inverse[0], ((1,), (0,))),
                            ((1,), (0,)),
                        )
                        for group, value in enumerate((block_inverse[0], cross_part, block_inverse[1])):
                            for kind, part in enumerate(split_three(value)):
                                at = half_tile * (3 * group + kind)
                                diag[panel, :, at : at + half_tile] = part

        return 0

    lax.fori_loop(0, lead // SUB, factor_step, 0)
    expand(low, diag, low_pieces, diag_first, diag_second)
    spread_points(points_rows[...], row_spread)
    covariance_loop(row_spread, lead_points, lead_table, cov_even, count, tile)
    covs = (cov_even, cov_odd)
    always = points_rows[0, 0] >= -1.0
    for t in range(panels):

        @pl.when(always)
        def _(t=t):
            ahead = Nothing()
            if t + 1 < panels:
                ahead = Ahead(row_spread, lead_points, lead_table, tile * (t + 1), covs[(t + 1) % 2])
            solve_block(t, covs[t % 2], low_pieces, diag_first, diag_second, residual, rows_pieces, ahead)

    for t in range(panels):
        at = 3 * tile * t
        lanes = slice(tile * t, tile * (t + 1))
        col_rows[:, lanes] = rows_pieces[0:tile, at : at + tile]
        shared_rows[:, lanes] = rows_pieces[tile : tile + shared * piece, at : at + tile]
        for slot in range(shared):
            rows = slice(tile + piece * slot, tile + piece * (slot + 1))
            panel_out[slot, :, lanes] = rows_pieces[rows, at : at + tile].astype(f32) + rows_pieces[
                rows, at + 2 * tile : at + 3 * tile
            ].astype(f32)


def rows_kernel(
    place,
    points_rows,
    points_next,
    lead_points,
    lead_table,
    col_points,
    col_table,
    low,
    diag,
    col_rows,
    panel_in,
    panel_out,
    trail_out,
    row_spread,
    low_pieces,
    diag_first,
    diag_second,
    cov_even,
    cov_odd,
    residual,
    rows_pieces,
):
    step = pl.program_id(0)
    tile = points_rows.shape[2]
    piece = panel_out.shape[1]
    panels = lead_points.shape[1] // tile
    row_index, col_index, row_count, target = place[0], place[1], place[2], place[3]
    row_tile = step * row_count + row_index
    covs = (cov_even, cov_odd)

    @pl.when(step == 0)
    def _():
        expand(low, diag, low_pieces, diag_first, diag_second)
        spread_points(points_rows[0], row_spread)
        covariance_loop(row_spread, lead_points, lead_table, cov_even, tile, tile)

    for t in range(panels):

        @pl.when(row_tile == t)
        def _(t=t):
            add_diagonal(covs[t % 2])

        @pl.when(step >= 0)
        def _(t=t):
            if t + 1 < panels:
                ahead = Ahead(row_spread, lead_points, lead_table, tile * (t + 1), covs[(t + 1) % 2])
            else:
                ahead = Ahead(row_spread, col_points, col_table, 0, covs[(t + 1) % 2])
            solve_block(t, covs[t % 2], low_pieces, diag_first, diag_second, residual, rows_pieces, ahead)

        @pl.when(row_tile <= t)
        def _(t=t):
            for order in (0, 1, 2):
                at = slice(tile * (3 * t + order), tile * (3 * t + order + 1))
                for start in range(0, tile, 128):
                    rows = slice(start, start + 128)
                    value = rows_pieces[rows, at]
                    row_id = lax.broadcasted_iota(jnp.int32, value.shape, 0) + start + row_tile * tile
                    col_id = lax.broadcasted_iota(jnp.int32, value.shape, 1) + t * tile
                    rows_pieces[rows, at] = jnp.where(col_id > row_id, jnp.zeros_like(value), value)

    last = covs[panels % 2]

    @pl.when(row_tile == target)
    def _():
        add_diagonal(last)

    @pl.when(step >= 0)
    def _():
        spread_points(points_next[0], row_spread)
        mine = pl.ds(pl.multiple_of(col_index * piece, piece), piece)
        ahead = Ahead(row_spread, lead_points, lead_table, 0, covs[0])
        for t in range(panels):
            at = 3 * tile * t
            high = rows_pieces[mine, at : at + tile].astype(f32)
            rest = rows_pieces[mine, at + 2 * tile : at + 3 * tile].astype(f32)
            panel_out[0, :, tile * t : tile * (t + 1)] = high + rest
        parts = row_parts(tile)
        for part in parts:
            update = None
            for t in range(panels):
                at = 3 * tile * t
                term = dot_nt(rows_pieces[part, at : at + tile], col_rows[:, tile * t : tile * (t + 1)])
                update = term if update is None else update + term
            ahead.share(0.5 / len(parts))
            trail_out[0, part, :] = last[part, :] - update
            ahead.share(0.5 / len(parts))
        ahead.share(1.0)


def trail_kernel(first, place, points_rows, col_points, col_table, rows, col_rows, trail_in, trail_out, row_spread):
    tile = points_rows.shape[2]
    spread_points(points_rows[0], row_spread)
    row_tile = (first + pl.program_id(0)) * place[2] + place[0]
    for part in row_parts(tile):
        update = dot_nt(rows[0, part, :], col_rows[...])
        for start in range(0, tile, 128):
            lanes = slice(start, start + 128)
            for row in range(part.start, part.stop, CHUNK):
                value = covariance(row_spread, slice(row, row + CHUNK), col_points, col_table, lanes)
                trail_out[0, row : row + CHUNK, lanes] = (
                    value - update[row - part.start : row - part.start + CHUNK, lanes]
                )

    @pl.when(row_tile == place[3])
    def _():
        add_diagonal(trail_out.at[0])


def local(grid_points, variable):
    slots, tile = variable.shape
    row_count = lax.axis_size("row")
    col_count = lax.axis_size("col")
    piece = tile // col_count
    row_index = lax.axis_index("row")
    col_index = lax.axis_index("col")
    lead = PANELS * tile
    half_tile = tile // 2
    shared = slots // SHARE
    kept = slots - shared
    used = -(-(PANELS + col_count) // row_count)
    own = jnp.concatenate([grid_points, variable[None]], 0)
    gathered = lax.all_gather(own[:, :used], "row", axis=2, tiled=True).reshape(3, -1)
    target = PANELS + col_index
    pad = lambda value: jnp.pad(value.astype(f32), ((0, 5), (0, 0)))
    lead_points = pad(gathered[:, :lead])
    col_values = lax.dynamic_slice_in_dim(gathered, target * tile, tile, 1)
    col_points = pad(col_values)
    lead_table = column_table(gathered[2, :lead])
    col_table = column_table(col_values[2])
    points_rows = jnp.pad(jnp.transpose(own, (1, 0, 2)).astype(f32), ((0, 0), (0, 5), (0, 0)))
    pieces = lax.dynamic_slice_in_dim(own[:, kept:], col_index * piece, piece, 2).reshape(3, shared * piece)
    first_rows = jnp.concatenate([col_values, pieces], 1).astype(f32)
    count = -(-first_rows.shape[1] // 128) * 128
    first_rows = jnp.pad(first_rows, ((0, 5), (0, count - first_rows.shape[1])))
    place = jnp.stack([row_index, col_index, jnp.int32(row_count), target]).astype(jnp.int32)
    whole = lambda shape: pl.BlockSpec(shape, lambda i, *s: (0,) * len(shape))
    panel_shape = jax.ShapeDtypeStruct((slots, piece, lead), f32)
    trail_shape = jax.ShapeDtypeStruct((slots, tile, tile), f32)
    low_shape = (lead - tile, 2 * (lead - tile))
    diag_shape = (PANELS, half_tile, 9 * half_tile)
    layout = [
        pltpu.VMEM((lead - tile, 3 * (lead - tile)), bf16),
        pltpu.VMEM((PANELS, half_tile, 6 * half_tile), bf16),
        pltpu.VMEM((PANELS, half_tile, 12 * half_tile), bf16),
    ]
    buffers = lambda rows: [
        pltpu.VMEM((rows, tile), f32),
        pltpu.VMEM((rows, tile), f32),
        pltpu.VMEM((rows, 12 * half_tile), bf16),
        pltpu.VMEM((rows, 3 * lead), bf16),
    ]
    params = pltpu.CompilerParams(dimension_semantics=("arbitrary",), vmem_limit_bytes=58 * 1024 * 1024)
    cost = lambda rows, size: pl.CostEstimate(flops=6 * rows * lead * lead, bytes_accessed=size, transcendentals=0)
    panel, low, diag, col_rows, shared_rows = pl.pallas_call(
        factor_kernel,
        out_shape=(
            panel_shape,
            jax.ShapeDtypeStruct(low_shape, bf16),
            jax.ShapeDtypeStruct(diag_shape, bf16),
            jax.ShapeDtypeStruct((tile, lead), bf16),
            jax.ShapeDtypeStruct((shared * piece, lead), bf16),
        ),
        grid=(1,),
        in_specs=[whole((8, count)), whole((8, lead)), whole((16, lead))],
        out_specs=(
            pl.BlockSpec((shared, piece, lead), lambda i: (SHARE - 1, 0, 0)),
            whole(low_shape),
            whole(diag_shape),
            whole((tile, lead)),
            whole((shared * piece, lead)),
        ),
        scratch_shapes=[pltpu.VMEM((lead, lead), f32), pltpu.VMEM((3, lead, 128), f32)]
        + layout
        + [
            pltpu.VMEM((lead, half_tile), bf16),
            pltpu.VMEM((lead, half_tile), bf16),
            pltpu.VMEM((2, SUB, SUB), f32),
            pltpu.VMEM((SUB, SUB), f32),
            pltpu.VMEM((2, half_tile, half_tile), f32),
            pltpu.VMEM((half_tile, half_tile), f32),
        ]
        + buffers(count),
        compiler_params=params,
        cost_estimate=cost(count + lead, 20 * tile * lead),
    )(first_rows, lead_points, lead_table)
    panel_half = lax.all_gather(shared_rows.reshape(shared, piece, lead), "col", axis=1, tiled=True)
    panel, trail = pl.pallas_call(
        rows_kernel,
        out_shape=(panel_shape, trail_shape),
        grid_spec=pltpu.PrefetchScalarGridSpec(
            num_scalar_prefetch=1,
            grid=(kept,),
            in_specs=[
                pl.BlockSpec((1, 8, tile), lambda i, s: (i, 0, 0)),
                pl.BlockSpec((1, 8, tile), lambda i, s: (jnp.minimum(i + 1, kept - 1), 0, 0)),
                whole((8, lead)),
                whole((16, lead)),
                whole((8, tile)),
                whole((16, tile)),
                whole(low_shape),
                whole(diag_shape),
                whole((tile, lead)),
                pl.BlockSpec(memory_space=pl.ANY),
            ],
            out_specs=[
                pl.BlockSpec((1, piece, lead), lambda i, s: (i, 0, 0)),
                pl.BlockSpec((1, tile, tile), lambda i, s: (i, 0, 0)),
            ],
            scratch_shapes=[pltpu.VMEM((3, tile, 128), f32)] + layout + buffers(tile),
        ),
        input_output_aliases={10: 0},
        compiler_params=params,
        cost_estimate=cost(kept * tile, 4 * kept * tile * (lead + tile)),
    )(place, points_rows, points_rows, lead_points, lead_table, col_points, col_table, low, diag, col_rows, panel)
    trail = pl.pallas_call(
        functools.partial(trail_kernel, kept),
        out_shape=trail_shape,
        grid_spec=pltpu.PrefetchScalarGridSpec(
            num_scalar_prefetch=1,
            grid=(shared,),
            in_specs=[
                pl.BlockSpec((1, 8, tile), lambda i, s: (kept + i, 0, 0)),
                whole((8, tile)),
                whole((16, tile)),
                pl.BlockSpec((1, tile, lead), lambda i, s: (i, 0, 0)),
                whole((tile, lead)),
                pl.BlockSpec(memory_space=pl.ANY),
            ],
            out_specs=pl.BlockSpec((1, tile, tile), lambda i, s: (kept + i, 0, 0)),
            scratch_shapes=[pltpu.VMEM((3, tile, 128), f32)],
        ),
        input_output_aliases={6: 0},
        compiler_params=params,
        cost_estimate=cost(shared * tile // 3, 4 * shared * tile * (lead + tile)),
    )(place, points_rows, col_points, col_table, panel_half, col_rows, trail)
    return panel, trail


def solution(mesh):
    return jax.shard_map(
        local,
        mesh=mesh,
        in_specs=(P(None, None, "row"), P(None, "row")),
        out_specs=(P(None, ("row", "col"), None), P(None, "row", "col")),
        check_vma=False,
    )
```

```python
import functools
import math

import jax
import jax.numpy as jnp
from jax import lax
from jax.experimental import pallas as pl
from jax.experimental.pallas import tpu as pltpu
from jax.sharding import PartitionSpec as P

PANELS = 3
GRID = 128
SUB = 128
CHUNK = 32
PART = 256
GROUP = 4
SHARED, SLOTS = 5, 12

range_scale = 0.05
nugget = 0.5
cross = ((1.0, 0.35, 0.2), (0.35, 1.0, 0.3), (0.2, 0.3, 1.0))
scales = (1.0, 1.3, 0.8)
series = (
    (1.0,),
    (1.0, 1.0),
    (1.0, 1.0, 1.0 / 3.0),
    (1.0, 1.0, 0.4, 1.0 / 15.0),
    (1.0, 1.0, 3.0 / 7.0, 2.0 / 21.0, 1.0 / 105.0),
)
log2e = 1.4426950408889634
step_scale = 1.0 / (GRID * range_scale)
f32 = jnp.float32
bf16 = jnp.bfloat16
NT = (((1,), (1,)), ((), ()))


def column_table(points, table):
    kinds = points[2:3, :]
    for kind in range(3):
        for power in range(5):
            values = []
            for other in range(3):
                terms = series[kind + other]
                base = cross[kind][other] * scales[kind] * scales[other]
                values.append(base * terms[power] * step_scale**power if power < len(terms) else 0.0)
            at = 5 * kind + power
            table[at : at + 1, :] = jnp.where(
                kinds == 0.0, values[0], jnp.where(kinds == 1.0, values[1], values[2])
            )


def dot_nt(left, right):
    return lax.dot_general(left, right, NT, preferred_element_type=f32)


def dot_full(left, right, dims):
    return lax.dot_general(
        left, right, (dims, ((), ())), precision=lax.Precision.HIGHEST, preferred_element_type=f32
    )


def split_two(value):
    high = value.astype(bf16)
    return high, (value - high.astype(f32)).astype(bf16)


def split_three(value):
    high = value.astype(bf16)
    rest = value - high.astype(f32)
    mid = rest.astype(bf16)
    return high, mid, (rest - mid.astype(f32)).astype(bf16)


def covariance(spread, rows, points, table, lanes):
    delta_x = spread[0, rows, :] - points[0:1, lanes]
    delta_y = spread[1, rows, :] - points[1:2, lanes]
    kind = spread[2, rows, :]
    square = delta_x * delta_x + delta_y * delta_y
    distance = square * lax.rsqrt(jnp.maximum(square, 1e-6))
    total = None
    for power in range(4, -1, -1):
        coef = jnp.where(
            kind == 0.0,
            table[power : power + 1, lanes],
            jnp.where(kind == 1.0, table[5 + power : 6 + power, lanes], table[10 + power : 11 + power, lanes]),
        )
        total = coef if total is None else total * distance + coef
    return total * jnp.exp2(distance * (-step_scale * log2e))


def spread_row(value, index):
    return jnp.broadcast_to(value[index : index + 1, :], value.shape)


def spread_lane(value, index):
    return jnp.broadcast_to(value[:, index : index + 1], value.shape)


def inverse_factor(groups):
    count = len(groups)
    shape = groups[0].shape
    lane = lax.broadcasted_iota(jnp.int32, shape, 1)
    sub = lax.broadcasted_iota(jnp.int32, shape, 0)
    result = []
    for block in range(count):
        own = groups[block]
        columns = [spread_lane(own, 8 * block + k) for k in range(8)]
        rows = [spread_row(own, k) for k in range(8)]
        tri = {(j, k): spread_row(columns[k], j) for j in range(8) for k in range(j, 8)}
        inverse = []
        for j in range(8):
            if j % 2 == 0:
                second = tri[j, j] * tri[j + 1, j + 1] - tri[j, j + 1] * tri[j, j + 1]
                inverse += [1.0 / tri[j, j], tri[j, j] * (1.0 / second)]
            rows[j] = jnp.where(lane == 8 * block + j, tri[j, j] + 1.0, rows[j])
            for k in range(j + 1, 8):
                factor = tri[j, k] * inverse[j]
                for m in range(k, 8):
                    tri[k, m] = tri[k, m] - factor * tri[j, m]
                rows[k] = rows[k] - factor * rows[j]
        for below in range(block + 1, count):
            column = [spread_lane(groups[below], 8 * block + k) for k in range(8)]
            value = groups[below]
            for j in range(8):
                factor = column[j] * inverse[j]
                for k in range(j + 1, 8):
                    column[k] = column[k] - factor * tri[j, k]
                value = value - factor * rows[j]
            groups[below] = value
        final, pivots = rows[0], inverse[0]
        for j in range(1, 8):
            final = jnp.where(sub == j, rows[j], final)
            pivots = jnp.where(sub == j, inverse[j], pivots)
        root = lax.sqrt(pivots)
        own_lane = 8 * block + sub
        result.append(jnp.where(lane > own_lane, 0.0, jnp.where(lane == own_lane, root, final * root)))
    return result


def spread_points(points, spread):
    rows = points.shape[1]
    turned = points[...].T
    for which in range(3):
        spread[which, 0:rows, :] = jnp.broadcast_to(turned[:, which : which + 1], (rows, 128))


def take_slot(own, slot, points):
    for which in range(3):
        points[which : which + 1, :] = own[which, pl.ds(slot, 1), :].astype(f32)


def take_columns(gathered, begin, points):
    for which in range(3):
        points[which : which + 1, :] = gathered[which : which + 1, pl.ds(begin, points.shape[1])].astype(f32)


def covariance_loop(spread, points, table, out, rows_count, width):
    def body(index, _):
        rows = pl.ds(pl.multiple_of(index * 128, 128), 128)
        for start in range(0, width, 128):
            out[rows, start : start + 128] = covariance(spread, rows, points, table, slice(start, start + 128))
        return 0

    lax.fori_loop(0, rows_count // 128, body, 0)


def add_diagonal(block):
    for start in range(0, block.shape[0], 128):
        here = slice(start, start + 128)
        row_id = lax.broadcasted_iota(jnp.int32, (128, 128), 0)
        col_id = lax.broadcasted_iota(jnp.int32, (128, 128), 1)
        block[here, here] = block[here, here] + jnp.where(row_id == col_id, nugget, 0.0)


class Ahead:
    def __init__(self, spread, points, table, begin, out):
        self.args = (spread, points, table, begin, out)
        rows, width = out.shape
        self.units = [
            (start, slice(row, row + CHUNK)) for start in range(0, width, 128) for row in range(0, rows, CHUNK)
        ]
        self.total = len(self.units)

    def share(self, part):
        spread, points, table, begin, out = self.args
        for _ in range(min(len(self.units), math.ceil(self.total * part))):
            start, rows = self.units.pop(0)
            out[rows, start : start + 128] = covariance(
                spread, rows, points, table, slice(begin + start, begin + start + 128)
            )


def row_parts(count):
    return [slice(start, min(start + PART, count)) for start in range(0, count, PART)]


def expand(low, diag, low_pieces, diag_first, diag_second):
    panels, half_tile, _ = diag_first.shape
    tile = 2 * half_tile
    rest_at = low.shape[1] // 2
    for panel in range(panels - 1):
        own = slice(tile * panel, tile * (panel + 1))
        other = slice(rest_at + tile * panel, rest_at + tile * (panel + 1))
        for order, source in enumerate((own, other, own)):
            at = tile * (3 * panel + order)
            low_pieces[tile * panel :, at : at + tile] = low[tile * panel :, source]
    for panel in range(panels):
        for order, kind in enumerate((0, 1, 2, 0, 1, 0)):
            for group in range(3):
                source = slice(half_tile * (3 * group + kind), half_tile * (3 * group + kind + 1))
                place = order if group == 0 else 6 * (group - 1) + order
                at = slice(half_tile * place, half_tile * (place + 1))
                (diag_first if group == 0 else diag_second)[panel, :, at] = diag[panel, :, source]


def solve_block(t, cov, low_pieces, diag_first, diag_second, residual, rows_pieces, ahead):
    panels, half_tile, _ = diag_first.shape
    tile = 2 * half_tile
    parts = row_parts(cov.shape[0])
    portion = 0.25 / len(parts)
    for part in parts:
        known = None
        if t:
            known = dot_nt(rows_pieces[part, 0 : 3 * tile * t], low_pieces[tile * (t - 1) : tile * t, 0 : 3 * tile * t])
        ahead.share(portion)
        for start in range(0, tile, 128):
            lanes = slice(start, start + 128)
            for row in range(part.start, part.stop, CHUNK):
                rows = slice(row, row + CHUNK)
                value = cov[rows, lanes]
                if t:
                    value = value - known[row - part.start : row - part.start + CHUNK, lanes]
                pieces = split_three(value)
                at = start if start < half_tile else start + 5 * half_tile
                for order, kind in enumerate((0, 0, 0, 1, 1, 2)):
                    residual[rows, at + half_tile * order : at + half_tile * order + 128] = pieces[kind]
        ahead.share(portion)
    for part in parts:
        for half, diag in enumerate((diag_first, diag_second)):
            solved = dot_nt(residual[part, 0 : 6 * half_tile * (half + 1)], diag[t])
            ahead.share(portion)
            high, rest = split_two(solved)
            at = 3 * tile * t + half_tile * half
            rows_pieces[part, at : at + half_tile] = high
            if t + 1 < panels:
                rows_pieces[part, at + tile : at + tile + half_tile] = high
            rows_pieces[part, at + 2 * tile : at + 2 * tile + half_tile] = rest
    ahead.share(1.0)


class Nothing:
    def share(self, part):
        pass


def factor_kernel(
    place,
    first_rows,
    gathered,
    panel_out,
    low,
    diag,
    col_rows,
    shared_rows,
    row_points,
    lead_points,
    lead_table,
    matrix,
    row_spread,
    low_pieces,
    diag_first,
    diag_second,
    step_high,
    step_rest,
    sub_inverse,
    sub_lower,
    block_inverse,
    block_lower,
    residual,
    rows_pieces,
):
    lead = lead_points.shape[1]
    tile = col_rows.shape[0]
    count = first_rows.shape[1]
    shared, piece, _ = panel_out.shape
    half_tile = tile // 2
    panels = lead // tile
    blocks = lead // half_tile
    rest_at = lead - tile
    take_columns(gathered, 0, lead_points)
    column_table(lead_points, lead_table)
    spread_points(lead_points, row_spread)
    for j in range(blocks):
        begin = half_tile * j

        def fill(index, _, begin=begin):
            at = pl.ds(pl.multiple_of(index * 128, 128), 128)
            for start in range(begin, begin + half_tile, 128):
                value = covariance(row_spread, at, lead_points, lead_table, slice(start, start + 128))
                row_id = lax.broadcasted_iota(jnp.int32, value.shape, 0) + index * 128
                col_id = lax.broadcasted_iota(jnp.int32, value.shape, 1) + start
                matrix[at, start : start + 128] = jnp.where(row_id == col_id, value + nugget, value)
            return 0

        lax.fori_loop(begin // 128, lead // 128, fill, 0)

    def factor_step(b, _):
        base = pl.multiple_of(b * SUB, SUB)
        here = pl.ds(base, SUB)
        result = inverse_factor([matrix[pl.ds(base + 8 * i, 8), here] for i in range(SUB // 8)])
        half = lax.rem(b, 2)
        for i in range(SUB // 8):
            sub_inverse[half, 8 * i : 8 * i + 8, :] = result[i]

        @pl.when(half == 0)
        def _():
            after = pl.ds(pl.multiple_of(base + SUB, SUB), SUB)
            lower = dot_full(matrix[after, here], sub_inverse[0], ((1,), (1,)))
            sub_lower[...] = lower
            matrix[after, after] = matrix[after, after] - dot_full(lower, lower, ((1,), (1,)))

        @pl.when(half == 1)
        def _():
            block = b // 2
            parity = lax.rem(block, 2)
            corner = -dot_full(
                sub_inverse[1],
                dot_full(sub_lower[...], sub_inverse[0], ((1,), (0,))),
                ((1,), (0,)),
            )
            inverse = jnp.concatenate(
                [
                    jnp.concatenate([sub_inverse[0], jnp.zeros((SUB, SUB), f32)], 1),
                    jnp.concatenate([corner, sub_inverse[1]], 1),
                ],
                0,
            )
            block_inverse[parity] = inverse
            high, mid = split_two(inverse)
            for which in range(blocks):

                @pl.when(block == which)
                def _(which=which):
                    begin = half_tile * (which + 1)
                    here = slice(half_tile * which, begin)
                    panel, odd = which // 2, which % 2
                    if begin < lead:
                        below_high, below_rest = split_two(matrix[begin:, here])
                        solved = dot_nt(below_high, high) + dot_nt(below_high, mid) + dot_nt(below_rest, high)
                        solved_high, solved_rest = split_two(solved)
                        step_high[begin:, :] = solved_high
                        step_rest[begin:, :] = solved_rest
                        for j in range(which + 1, blocks):
                            stripe = slice(half_tile * j, half_tile * (j + 1))
                            from_row = half_tile * j
                            matrix[from_row:, stripe] = matrix[from_row:, stripe] - (
                                dot_nt(step_high[from_row:, :], step_high[stripe, :])
                                + dot_nt(step_high[from_row:, :], step_rest[stripe, :])
                                + dot_nt(step_rest[from_row:, :], step_high[stripe, :])
                            )
                        if panel + 1 < panels:
                            later = slice(tile * (panel + 1), lead)
                            target = slice(tile * panel, lead - tile)
                            low[target, here] = step_high[later, :]
                            low[target, rest_at + here.start : rest_at + here.stop] = step_rest[later, :]
                        if odd == 0:
                            block_lower[...] = solved[0:half_tile, :]
                    if odd == 1:
                        cross_part = -dot_full(
                            block_inverse[1],
                            dot_full(block_lower[...], block_inverse[0], ((1,), (0,))),
                            ((1,), (0,)),
                        )
                        for group, value in enumerate((block_inverse[0], cross_part, block_inverse[1])):
                            for kind, part in enumerate(split_three(value)):
                                at = half_tile * (3 * group + kind)
                                diag[panel, :, at : at + half_tile] = part

        return 0

    lax.fori_loop(0, lead // SUB, factor_step, 0)
    expand(low, diag, low_pieces, diag_first, diag_second)
    row_points[0:3, :] = first_rows[...].astype(f32)
    spread_points(row_points, row_spread)
    covs = tuple(matrix.at[0:count, begin : begin + tile] for begin in (0, tile))
    covariance_loop(row_spread, lead_points, lead_table, covs[0], count, tile)
    always = place[0] >= 0
    for t in range(panels):

        @pl.when(always)
        def _(t=t):
            ahead = Nothing()
            if t + 1 < panels:
                ahead = Ahead(row_spread, lead_points, lead_table, tile * (t + 1), covs[(t + 1) % 2])
            solve_block(t, covs[t % 2], low_pieces, diag_first, diag_second, residual, rows_pieces, ahead)

    for t in range(panels):
        at = 3 * tile * t
        lanes = slice(tile * t, tile * (t + 1))
        col_rows[:, lanes] = rows_pieces[0:tile, at : at + tile]
        shared_rows[:, lanes] = rows_pieces[tile : tile + shared_rows.shape[0], at : at + tile]
        for slot in range(shared):
            begin = tile + shared_rows.shape[0] // shared * slot + place[1] // GROUP * piece
            rows = pl.ds(pl.multiple_of(begin, piece), piece)
            panel_out[slot, :, lanes] = rows_pieces[rows, at : at + tile].astype(f32) + rows_pieces[
                rows, at + 2 * tile : at + 3 * tile
            ].astype(f32)


def rows_kernel(
    place,
    own,
    gathered,
    low,
    diag,
    col_rows,
    panel_out,
    trail_out,
    row_points,
    lead_points,
    lead_table,
    col_points,
    col_table,
    row_spread,
    low_pieces,
    diag_first,
    diag_second,
    cov_even,
    cov_odd,
    residual,
    rows_pieces,
):
    step = pl.program_id(0)
    tile = row_points.shape[1]
    piece = panel_out.shape[1]
    panels = lead_points.shape[1] // tile
    row_index, col_index, row_count, target = place[0], place[1], place[2], place[3]
    row_tile = step * row_count + row_index
    covs = (cov_even, cov_odd)

    @pl.when(step == 0)
    def _():
        expand(low, diag, low_pieces, diag_first, diag_second)
        take_columns(gathered, 0, lead_points)
        column_table(lead_points, lead_table)
        take_columns(gathered, pl.multiple_of(target * tile, tile), col_points)
        column_table(col_points, col_table)
        take_slot(own, 0, row_points)
        spread_points(row_points, row_spread)
        covariance_loop(row_spread, lead_points, lead_table, cov_even, tile, tile)

    for t in range(panels):

        @pl.when(row_tile == t)
        def _(t=t):
            add_diagonal(covs[t % 2])

        @pl.when(step >= 0)
        def _(t=t):
            if t + 1 < panels:
                ahead = Ahead(row_spread, lead_points, lead_table, tile * (t + 1), covs[(t + 1) % 2])
            else:
                ahead = Ahead(row_spread, col_points, col_table, 0, covs[(t + 1) % 2])
            solve_block(t, covs[t % 2], low_pieces, diag_first, diag_second, residual, rows_pieces, ahead)

        @pl.when(row_tile <= t)
        def _(t=t):
            for order in (0, 1, 2):
                at = slice(tile * (3 * t + order), tile * (3 * t + order + 1))
                for start in range(0, tile, 128):
                    rows = slice(start, start + 128)
                    value = rows_pieces[rows, at]
                    row_id = lax.broadcasted_iota(jnp.int32, value.shape, 0) + start + row_tile * tile
                    col_id = lax.broadcasted_iota(jnp.int32, value.shape, 1) + t * tile
                    rows_pieces[rows, at] = jnp.where(col_id > row_id, jnp.zeros_like(value), value)

    last = covs[panels % 2]

    @pl.when(row_tile == target)
    def _():
        add_diagonal(last)

    @pl.when(step >= 0)
    def _():
        take_slot(own, jnp.minimum(step + 1, pl.num_programs(0) - 1), row_points)
        spread_points(row_points, row_spread)
        mine = pl.ds(pl.multiple_of(col_index * piece, piece), piece)
        ahead = Ahead(row_spread, lead_points, lead_table, 0, covs[0])
        for t in range(panels):
            at = 3 * tile * t
            high = rows_pieces[mine, at : at + tile].astype(f32)
            rest = rows_pieces[mine, at + 2 * tile : at + 3 * tile].astype(f32)
            panel_out[0, :, tile * t : tile * (t + 1)] = high + rest
        parts = row_parts(tile)
        for part in parts:
            update = None
            for t in range(panels):
                at = 3 * tile * t
                term = dot_nt(rows_pieces[part, at : at + tile], col_rows[:, tile * t : tile * (t + 1)])
                update = term if update is None else update + term
            ahead.share(0.5 / len(parts))
            trail_out[0, part, :] = last[part, :] - update
            ahead.share(0.5 / len(parts))
        ahead.share(1.0)


def trail_kernel(
    first,
    place,
    own,
    gathered,
    col_rows,
    panel,
    rows_0,
    rows_1,
    rows_2,
    rows_3,
    panel_in,
    trail_in,
    panel_out,
    trail_out,
    row_points,
    col_points,
    col_table,
    row_spread,
    rows,
):
    step = pl.program_id(0)
    tile = row_points.shape[1]
    _, groups, piece, _ = rows_0.shape

    @pl.when(step == 0)
    def _():
        take_columns(gathered, pl.multiple_of(place[3] * tile, tile), col_points)
        column_table(col_points, col_table)

    take_slot(own, first + step, row_points)
    spread_points(row_points, row_spread)
    row_tile = (first + step) * place[2] + place[0]
    mine = lax.rem(place[1], GROUP)
    for which, source in enumerate((rows_0, rows_1, rows_2, rows_3)):
        for group in range(groups):
            begin = (group * GROUP + jnp.bitwise_xor(mine, which)) * piece
            rows[pl.ds(pl.multiple_of(begin, piece), piece), :] = source[0, group]
    panel_out[...] = panel[...]
    for part in row_parts(tile):
        update = dot_nt(rows[part, :], col_rows[...])
        for start in range(0, tile, 128):
            lanes = slice(start, start + 128)
            for row in range(part.start, part.stop, CHUNK):
                value = covariance(row_spread, slice(row, row + CHUNK), col_points, col_table, lanes)
                trail_out[0, row : row + CHUNK, lanes] = (
                    value - update[row - part.start : row - part.start + CHUNK, lanes]
                )

    @pl.when(row_tile == place[3])
    def _():
        add_diagonal(trail_out.at[0])


def local(grid_points, variable):
    slots, tile = variable.shape
    row_count = lax.axis_size("row")
    col_count = lax.axis_size("col")
    piece = tile // col_count
    row_index = lax.axis_index("row")
    col_index = lax.axis_index("col")
    lead = PANELS * tile
    half_tile = tile // 2
    shared = slots * SHARED // SLOTS
    kept = slots - shared
    groups = col_count // GROUP
    used = -(-(PANELS + col_count) // row_count)
    own = jnp.concatenate([grid_points, variable[None]], 0)
    gathered = lax.all_gather(own[:, :used], "row", axis=2, tiled=True).reshape(3, -1)
    target = PANELS + col_index
    col_values = lax.dynamic_slice_in_dim(gathered, target * tile, tile, 1)
    pieces = own[:, kept:].reshape(3, shared, groups, GROUP, piece)
    pieces = lax.dynamic_index_in_dim(pieces, lax.rem(col_index, GROUP), 3, False).reshape(3, -1)
    exact = tile + pieces.shape[1]
    count = -(-exact // 128) * 128
    first_rows = jnp.concatenate([col_values, pieces, jnp.zeros((3, count - exact), jnp.int32)], 1)
    place = jnp.stack([row_index, col_index, jnp.int32(row_count), target]).astype(jnp.int32)
    whole = lambda shape: pl.BlockSpec(shape, lambda i, s: (0,) * len(shape), pipeline_mode=pl.Buffered(1))
    any_place = pl.BlockSpec(memory_space=pl.ANY)
    panel_shape = jax.ShapeDtypeStruct((slots, piece, lead), f32)
    trail_shape = jax.ShapeDtypeStruct((slots, tile, tile), f32)
    low_shape = (lead - tile, 2 * (lead - tile))
    diag_shape = (PANELS, half_tile, 9 * half_tile)
    exchange_shape = (shared, groups, piece, lead)
    points = lambda columns: [pltpu.VMEM((8, columns), f32), pltpu.VMEM((16, columns), f32)]
    layout = [
        pltpu.VMEM((lead - tile, 3 * (lead - tile)), bf16),
        pltpu.VMEM((PANELS, half_tile, 6 * half_tile), bf16),
        pltpu.VMEM((PANELS, half_tile, 12 * half_tile), bf16),
    ]
    buffers = lambda rows: [
        pltpu.VMEM((rows, tile), f32),
        pltpu.VMEM((rows, tile), f32),
        pltpu.VMEM((rows, 12 * half_tile), bf16),
        pltpu.VMEM((rows, 3 * lead), bf16),
    ]
    params = pltpu.CompilerParams(dimension_semantics=("arbitrary",), vmem_limit_bytes=60 * 1024 * 1024)
    cost = lambda rows, size: pl.CostEstimate(flops=6 * rows * lead * lead, bytes_accessed=size, transcendentals=0)
    panel_part, low, diag, col_rows, shared_rows = pl.pallas_call(
        factor_kernel,
        out_shape=(
            jax.ShapeDtypeStruct((shared, piece, lead), f32),
            jax.ShapeDtypeStruct(low_shape, bf16),
            jax.ShapeDtypeStruct(diag_shape, bf16),
            jax.ShapeDtypeStruct((tile, lead), bf16),
            jax.ShapeDtypeStruct((exact - tile, lead), bf16),
        ),
        grid_spec=pltpu.PrefetchScalarGridSpec(
            num_scalar_prefetch=1,
            grid=(1,),
            in_specs=[whole((3, count)), whole(gathered.shape)],
            out_specs=(
                whole((shared, piece, lead)),
                whole(low_shape),
                whole(diag_shape),
                whole((tile, lead)),
                whole((exact - tile, lead)),
            ),
            scratch_shapes=[pltpu.VMEM((8, count), f32)]
            + points(lead)
            + [pltpu.VMEM((lead, lead), f32), pltpu.VMEM((3, max(lead, count), 128), f32)]
            + layout
            + [
                pltpu.VMEM((lead, half_tile), bf16),
                pltpu.VMEM((lead, half_tile), bf16),
                pltpu.VMEM((2, SUB, SUB), f32),
                pltpu.VMEM((SUB, SUB), f32),
                pltpu.VMEM((2, half_tile, half_tile), f32),
                pltpu.VMEM((half_tile, half_tile), f32),
            ]
            + buffers(count)[2:],
        ),
        compiler_params=params,
        cost_estimate=cost(count + lead, 20 * tile * lead),
    )(place, first_rows, gathered)
    rows_0 = shared_rows.reshape(exchange_shape)
    others = [
        lax.ppermute(rows_0, "col", [(device, device ^ which) for device in range(col_count)])
        for which in range(1, GROUP)
    ]
    panel, trail = pl.pallas_call(
        rows_kernel,
        out_shape=(panel_shape, trail_shape),
        grid_spec=pltpu.PrefetchScalarGridSpec(
            num_scalar_prefetch=1,
            grid=(kept,),
            in_specs=[
                whole(own.shape),
                whole(gathered.shape),
                whole(low_shape),
                whole(diag_shape),
                whole((tile, lead)),
            ],
            out_specs=[
                pl.BlockSpec((1, piece, lead), lambda i, s: (i, 0, 0)),
                pl.BlockSpec((1, tile, tile), lambda i, s: (i, 0, 0)),
            ],
            scratch_shapes=[pltpu.VMEM((8, tile), f32)]
            + points(lead)
            + points(tile)
            + [pltpu.VMEM((3, tile, 128), f32)]
            + layout
            + buffers(tile),
        ),
        compiler_params=params,
        cost_estimate=cost(kept * tile, 4 * kept * tile * (lead + tile)),
    )(place, own, gathered, low, diag, col_rows)
    block = lambda shape: pl.BlockSpec((1,) + shape[1:], lambda i, s: (i,) + (0,) * (len(shape) - 1))
    later = lambda shape: pl.BlockSpec((1,) + shape[1:], lambda i, s: (kept + i,) + (0,) * (len(shape) - 1))
    return pl.pallas_call(
        functools.partial(trail_kernel, kept),
        out_shape=(panel_shape, trail_shape),
        grid_spec=pltpu.PrefetchScalarGridSpec(
            num_scalar_prefetch=1,
            grid=(shared,),
            in_specs=[whole(own.shape), whole(gathered.shape), whole((tile, lead)), block(panel_part.shape)]
            + [block(exchange_shape)] * GROUP
            + [any_place, any_place],
            out_specs=(later(panel_shape.shape), later(trail_shape.shape)),
            scratch_shapes=[pltpu.VMEM((8, tile), f32)]
            + points(tile)
            + [pltpu.VMEM((3, tile, 128), f32), pltpu.VMEM((tile, lead), bf16)],
        ),
        input_output_aliases={9: 0, 10: 1},
        compiler_params=params,
        cost_estimate=cost(shared * tile // 3, 4 * shared * tile * (lead + tile)),
    )(place, own, gathered, col_rows, panel_part, rows_0, *others, panel, trail)


def solution(mesh):
    return jax.shard_map(
        local,
        mesh=mesh,
        in_specs=(P(None, None, "row"), P(None, "row")),
        out_specs=(P(None, ("row", "col"), None), P(None, "row", "col")),
        check_vma=False,
    )
```

```python
import functools
import math

import jax
import jax.numpy as jnp
from jax import lax
from jax.experimental import pallas as pl
from jax.experimental.pallas import tpu as pltpu
from jax.sharding import PartitionSpec as P

PANELS = 3
GRID = 128
SUB = 128
CHUNK = 32
PART = 256
GROUP = 4
SHARED, SLOTS = 5, 12

range_scale = 0.05
nugget = 0.5
cross = ((1.0, 0.35, 0.2), (0.35, 1.0, 0.3), (0.2, 0.3, 1.0))
scales = (1.0, 1.3, 0.8)
series = (
    (1.0,),
    (1.0, 1.0),
    (1.0, 1.0, 1.0 / 3.0),
    (1.0, 1.0, 0.4, 1.0 / 15.0),
    (1.0, 1.0, 3.0 / 7.0, 2.0 / 21.0, 1.0 / 105.0),
)
log2e = 1.4426950408889634
step_scale = 1.0 / (GRID * range_scale)
f32 = jnp.float32
bf16 = jnp.bfloat16
NT = (((1,), (1,)), ((), ()))


def column_table(points, table):
    kinds = points[2:3, :]
    for kind in range(3):
        for power in range(5):
            values = []
            for other in range(3):
                terms = series[kind + other]
                base = cross[kind][other] * scales[kind] * scales[other]
                values.append(base * terms[power] * step_scale**power if power < len(terms) else 0.0)
            at = 5 * kind + power
            table[at : at + 1, :] = jnp.where(
                kinds == 0.0, values[0], jnp.where(kinds == 1.0, values[1], values[2])
            )


def dot_nt(left, right):
    return lax.dot_general(left, right, NT, preferred_element_type=f32)


def dot_full(left, right, dims):
    return lax.dot_general(
        left, right, (dims, ((), ())), precision=lax.Precision.HIGHEST, preferred_element_type=f32
    )


def split_two(value):
    high = value.astype(bf16)
    return high, (value - high.astype(f32)).astype(bf16)


def split_three(value):
    high = value.astype(bf16)
    rest = value - high.astype(f32)
    mid = rest.astype(bf16)
    return high, mid, (rest - mid.astype(f32)).astype(bf16)


def covariance(spread, rows, points, table, lanes):
    delta_x = spread[0, rows, :] - points[0:1, lanes]
    delta_y = spread[1, rows, :] - points[1:2, lanes]
    kind = spread[2, rows, :]
    square = delta_x * delta_x + delta_y * delta_y
    distance = square * lax.rsqrt(jnp.maximum(square, 1e-6))
    total = None
    for power in range(4, -1, -1):
        coef = jnp.where(
            kind == 0.0,
            table[power : power + 1, lanes],
            jnp.where(kind == 1.0, table[5 + power : 6 + power, lanes], table[10 + power : 11 + power, lanes]),
        )
        total = coef if total is None else total * distance + coef
    return total * jnp.exp2(distance * (-step_scale * log2e))


def spread_row(value, index):
    return jnp.broadcast_to(value[index : index + 1, :], value.shape)


def spread_lane(value, index):
    return jnp.broadcast_to(value[:, index : index + 1], value.shape)


def inverse_factor(groups):
    count = len(groups)
    shape = groups[0].shape
    lane = lax.broadcasted_iota(jnp.int32, shape, 1)
    sub = lax.broadcasted_iota(jnp.int32, shape, 0)
    result = []
    for block in range(count):
        own = groups[block]
        columns = [spread_lane(own, 8 * block + k) for k in range(8)]
        rows = [spread_row(own, k) for k in range(8)]
        tri = {(j, k): spread_row(columns[k], j) for j in range(8) for k in range(j, 8)}
        inverse = []
        for j in range(8):
            if j % 2 == 0:
                second = tri[j, j] * tri[j + 1, j + 1] - tri[j, j + 1] * tri[j, j + 1]
                inverse += [1.0 / tri[j, j], tri[j, j] * (1.0 / second)]
            rows[j] = jnp.where(lane == 8 * block + j, tri[j, j] + 1.0, rows[j])
            for k in range(j + 1, 8):
                factor = tri[j, k] * inverse[j]
                for m in range(k, 8):
                    tri[k, m] = tri[k, m] - factor * tri[j, m]
                rows[k] = rows[k] - factor * rows[j]
        for below in range(block + 1, count):
            column = [spread_lane(groups[below], 8 * block + k) for k in range(8)]
            value = groups[below]
            for j in range(8):
                factor = column[j] * inverse[j]
                for k in range(j + 1, 8):
                    column[k] = column[k] - factor * tri[j, k]
                value = value - factor * rows[j]
            groups[below] = value
        final, pivots = rows[0], inverse[0]
        for j in range(1, 8):
            final = jnp.where(sub == j, rows[j], final)
            pivots = jnp.where(sub == j, inverse[j], pivots)
        root = lax.sqrt(pivots)
        own_lane = 8 * block + sub
        result.append(jnp.where(lane > own_lane, 0.0, jnp.where(lane == own_lane, root, final * root)))
    return result


def spread_points(points, spread):
    rows = points.shape[1]
    turned = points[...].T
    for which in range(3):
        spread[which, 0:rows, :] = jnp.broadcast_to(turned[:, which : which + 1], (rows, 128))


def take_slot(own, slot, points):
    for which in range(3):
        points[which : which + 1, :] = own[which, pl.ds(slot, 1), :].astype(f32)


def take_columns(gathered, begin, points):
    for which in range(3):
        points[which : which + 1, :] = gathered[which : which + 1, pl.ds(begin, points.shape[1])].astype(f32)


def covariance_loop(spread, points, table, out, rows_count, width):
    def body(index, _):
        rows = pl.ds(pl.multiple_of(index * 128, 128), 128)
        for start in range(0, width, 128):
            out[rows, start : start + 128] = covariance(spread, rows, points, table, slice(start, start + 128))
        return 0

    lax.fori_loop(0, rows_count // 128, body, 0)


def add_diagonal(block):
    for start in range(0, block.shape[0], 128):
        here = slice(start, start + 128)
        row_id = lax.broadcasted_iota(jnp.int32, (128, 128), 0)
        col_id = lax.broadcasted_iota(jnp.int32, (128, 128), 1)
        block[here, here] = block[here, here] + jnp.where(row_id == col_id, nugget, 0.0)


class Ahead:
    def __init__(self, spread, points, table, begin, out):
        self.args = (spread, points, table, begin, out)
        rows, width = out.shape
        self.units = [
            (start, slice(row, row + CHUNK)) for start in range(0, width, 128) for row in range(0, rows, CHUNK)
        ]
        self.total = len(self.units)

    def share(self, part):
        spread, points, table, begin, out = self.args
        for _ in range(min(len(self.units), math.ceil(self.total * part))):
            start, rows = self.units.pop(0)
            out[rows, start : start + 128] = covariance(
                spread, rows, points, table, slice(begin + start, begin + start + 128)
            )


def row_parts(count):
    return [slice(start, min(start + PART, count)) for start in range(0, count, PART)]


def expand(low, diag, low_pieces, diag_first, diag_second):
    panels, half_tile, _ = diag_first.shape
    tile = 2 * half_tile
    rest_at = low.shape[1] // 2
    for panel in range(panels - 1):
        own = slice(tile * panel, tile * (panel + 1))
        other = slice(rest_at + tile * panel, rest_at + tile * (panel + 1))
        for order, source in enumerate((own, other, own)):
            at = tile * (3 * panel + order)
            low_pieces[tile * panel :, at : at + tile] = low[tile * panel :, source]
    for panel in range(panels):
        for order, kind in enumerate((0, 1, 2, 0, 1, 0)):
            for group in range(3):
                source = slice(half_tile * (3 * group + kind), half_tile * (3 * group + kind + 1))
                place = order if group == 0 else 6 * (group - 1) + order
                at = slice(half_tile * place, half_tile * (place + 1))
                (diag_first if group == 0 else diag_second)[panel, :, at] = diag[panel, :, source]


def solve_block(t, cov, low_pieces, diag_first, diag_second, residual, rows_pieces, ahead):
    panels, half_tile, _ = diag_first.shape
    tile = 2 * half_tile
    parts = row_parts(cov.shape[0])
    portion = 1.0 / (len(parts) * (12 * t + 18))
    for part in parts:
        known = None
        if t:
            known = dot_nt(rows_pieces[part, 0 : 3 * tile * t], low_pieces[tile * (t - 1) : tile * t, 0 : 3 * tile * t])
        ahead.share(12 * t * portion)
        for start in range(0, tile, 128):
            lanes = slice(start, start + 128)
            for row in range(part.start, part.stop, CHUNK):
                rows = slice(row, row + CHUNK)
                value = cov[rows, lanes]
                if t:
                    value = value - known[row - part.start : row - part.start + CHUNK, lanes]
                pieces = split_three(value)
                at = start if start < half_tile else start + 2 * half_tile
                for kind in range(3):
                    residual[rows, at + half_tile * kind : at + half_tile * kind + 128] = pieces[kind]
    for part in parts:
        for half, diag in enumerate((diag_first, diag_second)):
            left = [
                residual[part, half_tile * (3 * group + kind) : half_tile * (3 * group + kind + 1)]
                for group in range(half + 1)
                for kind in (0, 0, 0, 1, 1, 2)
            ]
            solved = dot_nt(jnp.concatenate(left, 1), diag[t])
            ahead.share(6 * (half + 1) * portion)
            high, rest = split_two(solved)
            at = 3 * tile * t + half_tile * half
            rows_pieces[part, at : at + half_tile] = high
            if t + 1 < panels:
                rows_pieces[part, at + tile : at + tile + half_tile] = high
            rows_pieces[part, at + 2 * tile : at + 2 * tile + half_tile] = rest
    ahead.share(1.0)


class Nothing:
    def share(self, part):
        pass


def factor_kernel(
    place,
    first_rows,
    gathered,
    panel_out,
    low,
    diag,
    col_rows,
    shared_rows,
    row_points,
    lead_points,
    lead_table,
    matrix,
    row_spread,
    low_pieces,
    diag_first,
    diag_second,
    step_high,
    step_rest,
    sub_inverse,
    sub_lower,
    block_inverse,
    block_lower,
    sub_product,
    residual,
    rows_pieces,
):
    lead = lead_points.shape[1]
    tile = col_rows.shape[0]
    count = first_rows.shape[1]
    shared, piece, _ = panel_out.shape
    half_tile = tile // 2
    panels = lead // tile
    blocks = lead // half_tile
    rest_at = lead - tile
    take_columns(gathered, 0, lead_points)
    column_table(lead_points, lead_table)
    spread_points(lead_points, row_spread)
    for j in range(blocks):
        begin = half_tile * j

        def fill(index, _, begin=begin):
            at = pl.ds(pl.multiple_of(index * 128, 128), 128)
            for start in range(begin, begin + half_tile, 128):
                value = covariance(row_spread, at, lead_points, lead_table, slice(start, start + 128))
                row_id = lax.broadcasted_iota(jnp.int32, value.shape, 0) + index * 128
                col_id = lax.broadcasted_iota(jnp.int32, value.shape, 1) + start
                matrix[at, start : start + 128] = jnp.where(row_id == col_id, value + nugget, value)
            return 0

        lax.fori_loop(begin // 128, lead // 128, fill, 0)

    def factor_step(b, _):
        base = pl.multiple_of(b * SUB, SUB)
        here = pl.ds(base, SUB)
        sub_product[...] = dot_full(sub_lower[...], sub_inverse[0], ((1,), (0,)))
        result = inverse_factor([matrix[pl.ds(base + 8 * i, 8), here] for i in range(SUB // 8)])
        half = lax.rem(b, 2)
        for i in range(SUB // 8):
            sub_inverse[half, 8 * i : 8 * i + 8, :] = result[i]

        @pl.when(half == 0)
        def _():
            after = pl.ds(pl.multiple_of(base + SUB, SUB), SUB)
            lower = dot_full(matrix[after, here], sub_inverse[0], ((1,), (1,)))
            sub_lower[...] = lower
            matrix[after, after] = matrix[after, after] - dot_full(lower, lower, ((1,), (1,)))

        @pl.when(half == 1)
        def _():
            block = b // 2
            parity = lax.rem(block, 2)
            corner = -dot_full(sub_inverse[1], sub_product[...], ((1,), (0,)))
            inverse = jnp.concatenate(
                [
                    jnp.concatenate([sub_inverse[0], jnp.zeros((SUB, SUB), f32)], 1),
                    jnp.concatenate([corner, sub_inverse[1]], 1),
                ],
                0,
            )
            block_inverse[parity] = inverse
            high, mid = split_two(inverse)
            for which in range(blocks):

                @pl.when(block == which)
                def _(which=which):
                    begin = half_tile * (which + 1)
                    here = slice(half_tile * which, begin)
                    panel, odd = which // 2, which % 2
                    if begin < lead:
                        below_high, below_rest = split_two(matrix[begin:, here])
                        solved = dot_nt(
                            jnp.concatenate([below_high, below_high, below_rest], 1),
                            jnp.concatenate([high, mid, high], 1),
                        )
                        solved_high, solved_rest = split_two(solved)
                        step_high[begin:, :] = solved_high
                        step_rest[begin:, :] = solved_rest
                        for j in range(which + 1, blocks):
                            stripe = slice(half_tile * j, half_tile * (j + 1))
                            from_row = half_tile * j
                            left_high, left_rest = step_high[from_row:, :], step_rest[from_row:, :]
                            right_high, right_rest = step_high[stripe, :], step_rest[stripe, :]
                            matrix[from_row:, stripe] = matrix[from_row:, stripe] - dot_nt(
                                jnp.concatenate([left_high, left_high, left_rest], 1),
                                jnp.concatenate([right_high, right_rest, right_high], 1),
                            )
                        if panel + 1 < panels:
                            later = slice(tile * (panel + 1), lead)
                            target = slice(tile * panel, lead - tile)
                            low[target, here] = step_high[later, :]
                            low[target, rest_at + here.start : rest_at + here.stop] = step_rest[later, :]
                        if odd == 0:
                            block_lower[...] = solved[0:half_tile, :]
                    if odd == 1:
                        cross_part = -dot_full(
                            block_inverse[1],
                            dot_full(block_lower[...], block_inverse[0], ((1,), (0,))),
                            ((1,), (0,)),
                        )
                        for group, value in enumerate((block_inverse[0], cross_part, block_inverse[1])):
                            for kind, part in enumerate(split_three(value)):
                                at = half_tile * (3 * group + kind)
                                diag[panel, :, at : at + half_tile] = part

        return 0

    lax.fori_loop(0, lead // SUB, factor_step, 0)
    expand(low, diag, low_pieces, diag_first, diag_second)
    row_points[0:3, :] = first_rows[...].astype(f32)
    spread_points(row_points, row_spread)
    covs = tuple(matrix.at[0:count, begin : begin + tile] for begin in (0, tile))
    covariance_loop(row_spread, lead_points, lead_table, covs[0], count, tile)
    always = place[0] >= 0
    for t in range(panels):

        @pl.when(always)
        def _(t=t):
            ahead = Nothing()
            if t + 1 < panels:
                ahead = Ahead(row_spread, lead_points, lead_table, tile * (t + 1), covs[(t + 1) % 2])
            solve_block(t, covs[t % 2], low_pieces, diag_first, diag_second, residual, rows_pieces, ahead)

    for t in range(panels):
        at = 3 * tile * t
        lanes = slice(tile * t, tile * (t + 1))
        col_rows[:, lanes] = rows_pieces[0:tile, at : at + tile]
        shared_rows[:, lanes] = rows_pieces[tile : tile + shared_rows.shape[0], at : at + tile]
        for slot in range(shared):
            begin = tile + shared_rows.shape[0] // shared * slot + place[1] // GROUP * piece
            rows = pl.ds(pl.multiple_of(begin, piece), piece)
            panel_out[slot, :, lanes] = rows_pieces[rows, at : at + tile].astype(f32) + rows_pieces[
                rows, at + 2 * tile : at + 3 * tile
            ].astype(f32)


def rows_kernel(
    place,
    own,
    gathered,
    low,
    diag,
    col_rows,
    panel_out,
    trail_out,
    row_points,
    lead_points,
    lead_table,
    col_points,
    col_table,
    row_spread,
    low_pieces,
    diag_first,
    diag_second,
    cov_even,
    cov_odd,
    residual,
    rows_pieces,
):
    step = pl.program_id(0)
    tile = row_points.shape[1]
    piece = panel_out.shape[1]
    panels = lead_points.shape[1] // tile
    row_index, col_index, row_count, target = place[0], place[1], place[2], place[3]
    row_tile = step * row_count + row_index
    covs = (cov_even, cov_odd)

    @pl.when(step == 0)
    def _():
        expand(low, diag, low_pieces, diag_first, diag_second)
        take_columns(gathered, 0, lead_points)
        column_table(lead_points, lead_table)
        take_columns(gathered, pl.multiple_of(target * tile, tile), col_points)
        column_table(col_points, col_table)
        take_slot(own, 0, row_points)
        spread_points(row_points, row_spread)
        covariance_loop(row_spread, lead_points, lead_table, cov_even, tile, tile)

    for t in range(panels):

        @pl.when(row_tile == t)
        def _(t=t):
            add_diagonal(covs[t % 2])

        @pl.when(step >= 0)
        def _(t=t):
            if t + 1 < panels:
                ahead = Ahead(row_spread, lead_points, lead_table, tile * (t + 1), covs[(t + 1) % 2])
            else:
                ahead = Ahead(row_spread, col_points, col_table, 0, covs[(t + 1) % 2])
            solve_block(t, covs[t % 2], low_pieces, diag_first, diag_second, residual, rows_pieces, ahead)

        @pl.when(row_tile <= t)
        def _(t=t):
            for order in (0, 1, 2):
                at = slice(tile * (3 * t + order), tile * (3 * t + order + 1))
                for start in range(0, tile, 128):
                    rows = slice(start, start + 128)
                    value = rows_pieces[rows, at]
                    row_id = lax.broadcasted_iota(jnp.int32, value.shape, 0) + start + row_tile * tile
                    col_id = lax.broadcasted_iota(jnp.int32, value.shape, 1) + t * tile
                    rows_pieces[rows, at] = jnp.where(col_id > row_id, jnp.zeros_like(value), value)

    last = covs[panels % 2]

    @pl.when(row_tile == target)
    def _():
        add_diagonal(last)

    @pl.when(step >= 0)
    def _():
        take_slot(own, jnp.minimum(step + 1, pl.num_programs(0) - 1), row_points)
        spread_points(row_points, row_spread)
        mine = pl.ds(pl.multiple_of(col_index * piece, piece), piece)
        ahead = Ahead(row_spread, lead_points, lead_table, 0, covs[0])
        for t in range(panels):
            at = 3 * tile * t
            high = rows_pieces[mine, at : at + tile].astype(f32)
            rest = rows_pieces[mine, at + 2 * tile : at + 3 * tile].astype(f32)
            panel_out[0, :, tile * t : tile * (t + 1)] = high + rest
        parts = row_parts(tile)
        for part in parts:
            update = dot_nt(
                jnp.concatenate(
                    [rows_pieces[part, 3 * tile * t : 3 * tile * t + tile] for t in range(panels)], 1
                ),
                col_rows[...],
            )
            ahead.share(0.5 / len(parts))
            trail_out[0, part, :] = last[part, :] - update
            ahead.share(0.5 / len(parts))
        ahead.share(1.0)


def trail_kernel(
    first,
    place,
    own,
    gathered,
    col_rows,
    panel,
    rows_0,
    rows_1,
    rows_2,
    rows_3,
    panel_in,
    trail_in,
    panel_out,
    trail_out,
    row_points,
    col_points,
    col_table,
    row_spread,
    rows,
):
    step = pl.program_id(0)
    tile = row_points.shape[1]
    _, groups, piece, _ = rows_0.shape

    @pl.when(step == 0)
    def _():
        take_columns(gathered, pl.multiple_of(place[3] * tile, tile), col_points)
        column_table(col_points, col_table)

    take_slot(own, first + step, row_points)
    spread_points(row_points, row_spread)
    row_tile = (first + step) * place[2] + place[0]
    mine = lax.rem(place[1], GROUP)
    for which, source in enumerate((rows_0, rows_1, rows_2, rows_3)):
        for group in range(groups):
            begin = (group * GROUP + jnp.bitwise_xor(mine, which)) * piece
            rows[pl.ds(pl.multiple_of(begin, piece), piece), :] = source[0, group]
    panel_out[...] = panel[...]
    for part in row_parts(tile):
        update = dot_nt(rows[part, :], col_rows[...])
        for start in range(0, tile, 128):
            lanes = slice(start, start + 128)
            for row in range(part.start, part.stop, CHUNK):
                value = covariance(row_spread, slice(row, row + CHUNK), col_points, col_table, lanes)
                trail_out[0, row : row + CHUNK, lanes] = (
                    value - update[row - part.start : row - part.start + CHUNK, lanes]
                )

    @pl.when(row_tile == place[3])
    def _():
        add_diagonal(trail_out.at[0])


def local(grid_points, variable):
    slots, tile = variable.shape
    row_count = lax.axis_size("row")
    col_count = lax.axis_size("col")
    piece = tile // col_count
    row_index = lax.axis_index("row")
    col_index = lax.axis_index("col")
    lead = PANELS * tile
    half_tile = tile // 2
    shared = slots * SHARED // SLOTS
    kept = slots - shared
    groups = col_count // GROUP
    used = -(-(PANELS + col_count) // row_count)
    own = jnp.concatenate([grid_points, variable[None]], 0)
    gathered = lax.all_gather(own[:, :used], "row", axis=2, tiled=True).reshape(3, -1)
    target = PANELS + col_index
    col_values = lax.dynamic_slice_in_dim(gathered, target * tile, tile, 1)
    pieces = own[:, kept:].reshape(3, shared, groups, GROUP, piece)
    pieces = lax.dynamic_index_in_dim(pieces, lax.rem(col_index, GROUP), 3, False).reshape(3, -1)
    exact = tile + pieces.shape[1]
    count = -(-exact // 128) * 128
    first_rows = jnp.concatenate([col_values, pieces, jnp.zeros((3, count - exact), jnp.int32)], 1)
    place = jnp.stack([row_index, col_index, jnp.int32(row_count), target]).astype(jnp.int32)
    whole = lambda shape: pl.BlockSpec(shape, lambda i, s: (0,) * len(shape), pipeline_mode=pl.Buffered(1))
    any_place = pl.BlockSpec(memory_space=pl.ANY)
    panel_shape = jax.ShapeDtypeStruct((slots, piece, lead), f32)
    trail_shape = jax.ShapeDtypeStruct((slots, tile, tile), f32)
    low_shape = (lead - tile, 2 * (lead - tile))
    diag_shape = (PANELS, half_tile, 9 * half_tile)
    exchange_shape = (shared, groups, piece, lead)
    points = lambda columns: [pltpu.VMEM((8, columns), f32), pltpu.VMEM((16, columns), f32)]
    layout = [
        pltpu.VMEM((lead - tile, 3 * (lead - tile)), bf16),
        pltpu.VMEM((PANELS, half_tile, 6 * half_tile), bf16),
        pltpu.VMEM((PANELS, half_tile, 12 * half_tile), bf16),
    ]
    buffers = lambda rows: [
        pltpu.VMEM((rows, tile), f32),
        pltpu.VMEM((rows, tile), f32),
        pltpu.VMEM((rows, 6 * half_tile), bf16),
        pltpu.VMEM((rows, 3 * lead), bf16),
    ]
    params = pltpu.CompilerParams(dimension_semantics=("arbitrary",), vmem_limit_bytes=60 * 1024 * 1024)
    cost = lambda rows, size: pl.CostEstimate(flops=6 * rows * lead * lead, bytes_accessed=size, transcendentals=0)
    panel_part, low, diag, col_rows, shared_rows = pl.pallas_call(
        factor_kernel,
        out_shape=(
            jax.ShapeDtypeStruct((shared, piece, lead), f32),
            jax.ShapeDtypeStruct(low_shape, bf16),
            jax.ShapeDtypeStruct(diag_shape, bf16),
            jax.ShapeDtypeStruct((tile, lead), bf16),
            jax.ShapeDtypeStruct((exact - tile, lead), bf16),
        ),
        grid_spec=pltpu.PrefetchScalarGridSpec(
            num_scalar_prefetch=1,
            grid=(1,),
            in_specs=[whole((3, count)), whole(gathered.shape)],
            out_specs=(
                whole((shared, piece, lead)),
                whole(low_shape),
                whole(diag_shape),
                whole((tile, lead)),
                whole((exact - tile, lead)),
            ),
            scratch_shapes=[pltpu.VMEM((8, count), f32)]
            + points(lead)
            + [pltpu.VMEM((lead, lead), f32), pltpu.VMEM((3, max(lead, count), 128), f32)]
            + layout
            + [
                pltpu.VMEM((lead, half_tile), bf16),
                pltpu.VMEM((lead, half_tile), bf16),
                pltpu.VMEM((2, SUB, SUB), f32),
                pltpu.VMEM((SUB, SUB), f32),
                pltpu.VMEM((2, half_tile, half_tile), f32),
                pltpu.VMEM((half_tile, half_tile), f32),
                pltpu.VMEM((SUB, SUB), f32),
            ]
            + buffers(count)[2:],
        ),
        compiler_params=params,
        cost_estimate=cost(count + lead, 20 * tile * lead),
    )(place, first_rows, gathered)
    rows_0 = shared_rows.reshape(exchange_shape)
    others = [
        lax.ppermute(rows_0, "col", [(device, device ^ which) for device in range(col_count)])
        for which in range(1, GROUP)
    ]
    panel, trail = pl.pallas_call(
        rows_kernel,
        out_shape=(panel_shape, trail_shape),
        grid_spec=pltpu.PrefetchScalarGridSpec(
            num_scalar_prefetch=1,
            grid=(kept,),
            in_specs=[
                whole(own.shape),
                whole(gathered.shape),
                whole(low_shape),
                whole(diag_shape),
                whole((tile, lead)),
            ],
            out_specs=[
                pl.BlockSpec((1, piece, lead), lambda i, s: (i, 0, 0)),
                pl.BlockSpec((1, tile, tile), lambda i, s: (i, 0, 0)),
            ],
            scratch_shapes=[pltpu.VMEM((8, tile), f32)]
            + points(lead)
            + points(tile)
            + [pltpu.VMEM((3, tile, 128), f32)]
            + layout
            + buffers(tile),
        ),
        compiler_params=params,
        cost_estimate=cost(kept * tile, 4 * kept * tile * (lead + tile)),
    )(place, own, gathered, low, diag, col_rows)
    block = lambda shape: pl.BlockSpec((1,) + shape[1:], lambda i, s: (i,) + (0,) * (len(shape) - 1))
    later = lambda shape: pl.BlockSpec((1,) + shape[1:], lambda i, s: (kept + i,) + (0,) * (len(shape) - 1))
    return pl.pallas_call(
        functools.partial(trail_kernel, kept),
        out_shape=(panel_shape, trail_shape),
        grid_spec=pltpu.PrefetchScalarGridSpec(
            num_scalar_prefetch=1,
            grid=(shared,),
            in_specs=[whole(own.shape), whole(gathered.shape), whole((tile, lead)), block(panel_part.shape)]
            + [block(exchange_shape)] * GROUP
            + [any_place, any_place],
            out_specs=(later(panel_shape.shape), later(trail_shape.shape)),
            scratch_shapes=[pltpu.VMEM((8, tile), f32)]
            + points(tile)
            + [pltpu.VMEM((3, tile, 128), f32), pltpu.VMEM((tile, lead), bf16)],
        ),
        input_output_aliases={9: 0, 10: 1},
        compiler_params=params,
        cost_estimate=cost(shared * tile // 3, 4 * shared * tile * (lead + tile)),
    )(place, own, gathered, col_rows, panel_part, rows_0, *others, panel, trail)


def solution(mesh):
    return jax.shard_map(
        local,
        mesh=mesh,
        in_specs=(P(None, None, "row"), P(None, "row")),
        out_specs=(P(None, ("row", "col"), None), P(None, "row", "col")),
        check_vma=False,
    )
```
